32 devices in a mesh: dp: 16 (over z, x, core), mp: 2 (over y).
Axes of the slice: x: 2, y: 2, z: 4, core: 2. Of those that a mesh axis runs over, the one named last changes fastest.
Arguments:
- tokens: bfloat16 [2, 1024, 1024], P(None, 'dp'), may hold values from -6 to 6
- cotangent: bfloat16 [2, 1024, 1024], P(None, 'dp'), may hold values from -6 to 6
- segments: int32 [2, 1024], P(None, 'dp'), may hold values from 0 to 63, as said below
- w_qkv: float32 [3, 1024, 1024], P(None, 'dp', 'mp'), may hold values from -0.1875 to 0.1875
- w_out: float32 [1024, 1024], P('mp', 'dp'), may hold values from -0.75 to 0.75
- w_fc: float32 [1024, 4096], P('dp', 'mp'), may hold values from -0.1875 to 0.1875
- w_proj: float32 [4096, 1024], P('mp', 'dp'), may hold values from -0.09375 to 0.09375
- vec_norm: float32 [6, 1024], P(None, 'dp'), may hold values from -0.8 to 1.4, as said below
- vec_split: float32 [6, 1024], P(None, ('mp', 'dp')), may hold values from -1.2 to 1.2
- first_qkv: float32 [3, 1024, 1024], P(None, 'dp', 'mp'), may hold values from -32 to 32
- first_out: float32 [1024, 1024], P('mp', 'dp'), may hold values from -6 to 6
- first_fc: float32 [1024, 4096], P('dp', 'mp'), may hold values from -8 to 8
- first_proj: float32 [4096, 1024], P('mp', 'dp'), may hold values from -20 to 20
- first_norm: float32 [6, 1024], P(None, 'dp'), may hold values from -32 to 32
- first_split: float32 [6, 1024], P(None, ('mp', 'dp')), may hold values from -16 to 16
- second_qkv: float32 [3, 1024, 1024], P(None, 'dp', 'mp'), may hold values from 108.544 to 430.08
- second_out: float32 [1024, 1024], P('mp', 'dp'), may hold values from 4.3008 to 17.2032
- second_fc: float32 [1024, 4096], P('dp', 'mp'), may hold values from 9.8304 to 38.912
- second_proj: float32 [4096, 1024], P('mp', 'dp'), may hold values from 45.056 to 182.272
- second_norm: float32 [6, 1024], P(None, 'dp'), may hold values from 108.544 to 430.08
- second_split: float32 [6, 1024], P(None, ('mp', 'dp')), may hold values from 38.912 to 155.648
Outputs:
- out_tokens: bfloat16 [2, 1024, 1024], P(None, 'dp')
- in_grad: bfloat16 [2, 1024, 1024], P(None, 'dp')
- next_qkv: float32 [3, 1024, 1024], P(None, 'dp', 'mp')
- next_out: float32 [1024, 1024], P('mp', 'dp')
- next_fc: float32 [1024, 4096], P('dp', 'mp')
- next_proj: float32 [4096, 1024], P('mp', 'dp')
- next_norm: float32 [6, 1024], P(None, 'dp')
- next_split: float32 [6, 1024], P(None, ('mp', 'dp'))
- moment_qkv: float32 [3, 1024, 1024], P(None, 'dp', 'mp')
- moment_out: float32 [1024, 1024], P('mp', 'dp')
- moment_fc: float32 [1024, 4096], P('dp', 'mp')
- moment_proj: float32 [4096, 1024], P('mp', 'dp')
- moment_norm: float32 [6, 1024], P(None, 'dp')
- moment_split: float32 [6, 1024], P(None, ('mp', 'dp'))
- square_qkv: float32 [3, 1024, 1024], P(None, 'dp', 'mp')
- square_out: float32 [1024, 1024], P('mp', 'dp')
- square_fc: float32 [1024, 4096], P('dp', 'mp')
- square_proj: float32 [4096, 1024], P('mp', 'dp')
- square_norm: float32 [6, 1024], P(None, 'dp')
- square_split: float32 [6, 1024], P(None, ('mp', 'dp'))
The draws below stay inside these ranges and needn't reach their ends.
Inputs may be any that keep to these rules, and one draw needn't show every extreme that they name: `segments`: within each block of 64 positions (one micro-batch, one index of dp) the numbers start at 0, never fall and rise by at most one from a position to the next; equal numbers in a block form one sequence. In every draw some block holds a single sequence, and another block holds 64 sequences of one token. `vec_norm`: rows 0 and 2 are norm gains near one; the other rows are biases.
All inputs are finite; a program needn't handle non-finite values.
Results may differ from the reference program's by a relative error of at most 0.015.
Values may be sent and summed in bfloat16 or wider, within the bound.
A program may use at most 128 MiB of HBM per device.

```python
import math
import jax
import jax.numpy as jnp
from jax import lax

D = 1024
H = 16
HD = 64
FF = 4096
TOK_MB = 64
MB = 2
STEP = 10
TOKENS_MB = 1024
N_DP = 16


def draw_segments(key, part):
    key = jax.random.fold_in(key, 7)
    key_starts, key_whole, key_other = jax.random.split(key, 3)
    shape = (MB, N_DP, TOK_MB)
    total_blocks = MB * N_DP
    odds = max(2, min(48, TOK_MB // 2))
    starts = jax.random.randint(key_starts, shape, 0, odds) == 0
    position = lax.broadcasted_iota(jnp.int32, shape, 2)
    block_index = lax.broadcasted_iota(jnp.int32, shape, 0) * N_DP + lax.broadcasted_iota(jnp.int32, shape, 1)
    whole_block = jax.random.randint(key_whole, (), 0, total_blocks)
    single_block = (whole_block + 1 + jax.random.randint(key_other, (), 0, total_blocks - 1)) % total_blocks
    starts = starts | (block_index == single_block)
    starts = starts & (position > 0) & (block_index != whole_block)
    numbers = jnp.cumsum(starts.astype(jnp.int32), axis=2)
    return numbers.reshape(MB, N_DP * TOK_MB).astype(jnp.int32)


def draw_vec_norm(key, part):
    key = jax.random.fold_in(key, 5)
    noise_values = jnp.clip(jax.random.normal(key, (6, D), jnp.float32), -3.5, 3.5)
    row_index = lax.broadcasted_iota(jnp.int32, (6, D), 0)
    gain_rows = (row_index == 0) | (row_index == 2)
    return jnp.where(gain_rows, 1.0 + 0.1 * noise_values, 0.2 * noise_values).astype(jnp.float32)


def level_of(own_key, dims, cuts, low, top_value):
    loudness = 1.0
    for dim, blocks in cuts:
        draws = jax.random.uniform(jax.random.fold_in(jax.random.fold_in(own_key, 6), dim), (blocks,), jnp.float32, low / len(cuts), top_value / len(cuts))
        loudness = loudness * jnp.repeat(jnp.exp(draws), dims[dim] // blocks).reshape((-1,) + (1,) * (len(dims) - 1 - dim))
    return loudness


def normal_values(key, shape, deviation, most, cuts=(), kind=jnp.bfloat16):
    drawn = jax.random.normal(key, shape, jnp.float32) * deviation
    if len(cuts) > 0:
        drawn = level_of(key, shape, cuts, -0.22, 0.18) * drawn
    return jnp.clip(drawn, min=-most, max=most).astype(kind)


def setup_inputs(seed: int = 0) -> dict:
    seeds = jax.random.split(jax.random.key(seed), 22)
    tokens = normal_values(seeds[0], (MB, TOKENS_MB, D), 1.0, 6.0, ((1, 16),))
    cotangent = normal_values(seeds[1], (MB, TOKENS_MB, D), 1.0, 6.0, ((1, 16),))
    segments = draw_segments(jax.random.fold_in(seeds[21], 71), 0)
    w_qkv = normal_values(seeds[3], (3, D, D), D ** -0.5, 0.1875, ((1, 16), (2, 2)), jnp.float32)
    w_out = normal_values(seeds[4], (D, D), (D // min(32, max(2, TOK_MB // 4))) ** -0.5, 0.75, ((0, 2), (1, 16)), jnp.float32)
    w_fc = normal_values(seeds[5], (D, FF), D ** -0.5, 0.1875, ((0, 16), (1, 2)), jnp.float32)
    w_proj = normal_values(seeds[6], (FF, D), FF ** -0.5, 0.09375, ((0, 2), (1, 16)), jnp.float32)
    vec_norm = draw_vec_norm(jax.random.fold_in(seeds[21], 71), 0)
    vec_split = normal_values(seeds[8], (6, D), 0.2, 1.2, ((1, 32),), jnp.float32)
    first_qkv = normal_values(seeds[9], (3, D, D), (0.11 * (MB * TOK_MB * N_DP) ** 0.5), 32.0, ((1, 16), (2, 2)), jnp.float32)
    first_out = normal_values(seeds[10], (D, D), (0.022 * (MB * TOK_MB * N_DP) ** 0.5), 6.0, ((0, 2), (1, 16)), jnp.float32)
    first_fc = normal_values(seeds[11], (D, FF), (0.033 * (MB * TOK_MB * N_DP) ** 0.5), 8.0, ((0, 16), (1, 2)), jnp.float32)
    first_proj = normal_values(seeds[12], (FF, D), (0.072 * (MB * TOK_MB * N_DP) ** 0.5), 20.0, ((0, 2), (1, 16)), jnp.float32)
    first_norm = normal_values(seeds[13], (6, D), (0.11 * (MB * TOK_MB * N_DP) ** 0.5), 32.0, ((1, 16),), jnp.float32)
    first_split = normal_values(seeds[14], (6, D), (0.066 * (MB * TOK_MB * N_DP) ** 0.5), 16.0, ((1, 32),), jnp.float32)
    second_qkv = jnp.clip(jnp.exp(math.log(430.08) - 1.3768156 * jax.random.uniform(seeds[15], (3, D, D), jnp.float32) ** level_of(seeds[15], (3, D, D), ((1, 16), (2, 2)), -0.2, 0.2)), 108.544, 430.08)
    second_out = jnp.clip(jnp.exp(math.log(17.2032) - 1.3862944 * jax.random.uniform(seeds[16], (D, D), jnp.float32) ** level_of(seeds[16], (D, D), ((0, 2), (1, 16)), -0.2, 0.2)), 4.3008, 17.2032)
    second_fc = jnp.clip(jnp.exp(math.log(38.912) - 1.375823 * jax.random.uniform(seeds[17], (D, FF), jnp.float32) ** level_of(seeds[17], (D, FF), ((0, 16), (1, 2)), -0.2, 0.2)), 9.8304, 38.912)
    second_proj = jnp.clip(jnp.exp(math.log(182.272) - 1.397594 * jax.random.uniform(seeds[18], (FF, D), jnp.float32) ** level_of(seeds[18], (FF, D), ((0, 2), (1, 16)), -0.2, 0.2)), 45.056, 182.272)
    second_norm = jnp.clip(jnp.exp(math.log(430.08) - 1.3768156 * jax.random.uniform(seeds[19], (6, D), jnp.float32) ** level_of(seeds[19], (6, D), ((1, 16),), -0.2, 0.2)), 108.544, 430.08)
    second_split = jnp.clip(jnp.exp(math.log(155.648) - 1.3862944 * jax.random.uniform(seeds[20], (6, D), jnp.float32) ** level_of(seeds[20], (6, D), ((1, 32),), -0.2, 0.2)), 38.912, 155.648)
    return {"tokens": tokens, "cotangent": cotangent, "segments": segments, "w_qkv": w_qkv, "w_out": w_out, "w_fc": w_fc, "w_proj": w_proj, "vec_norm": vec_norm, "vec_split": vec_split, "first_qkv": first_qkv, "first_out": first_out, "first_fc": first_fc, "first_proj": first_proj, "first_norm": first_norm, "first_split": first_split, "second_qkv": second_qkv, "second_out": second_out, "second_fc": second_fc, "second_proj": second_proj, "second_norm": second_norm, "second_split": second_split}


@jax.custom_vjp
def low(v):
    return lax.optimization_barrier(v.astype(jnp.bfloat16)).astype(jnp.float32)

@jax.custom_vjp
def low_back(v):
    return v

def low_keep(v):
    return (low(v), None)

def low_pass(kept, grad):
    return (grad,)

def back_keep(v):
    return (v, None)

def back_low(kept, grad):
    return (low(grad),)
low.defvjp(low_keep, low_pass)
low_back.defvjp(back_keep, back_low)

def layer_norm(values, gain_row, shift_row):
    center = values - lax.optimization_barrier(jnp.mean(values, axis=-1, keepdims=True))
    spread = lax.optimization_barrier(jnp.mean(center * center, axis=-1, keepdims=True))
    return center * lax.rsqrt(spread + 1e-05) * gain_row + shift_row

def product(left, right):
    return jnp.dot(left, right, precision=lax.Precision.HIGHEST)

def rate_list():
    narrow = D // min(32, max(2, TOK_MB // 4))
    return (2.0 / math.sqrt(D), 2.0 / math.sqrt(narrow), 2.0 / math.sqrt(D), 2.0 / math.sqrt(FF), 0.8, 0.4)

def adamw(weight, gradient, first_moment, second, step_rate, weight_decay):
    first_new = 0.9 * first_moment + 0.1 * gradient
    second_new = 0.95 * second + 0.05 * gradient * gradient
    scaled_first = first_new / (1.0 - 0.9 ** STEP)
    scaled_second = second_new / (1.0 - 0.95 ** STEP)
    weight_new = weight - step_rate * (scaled_first / (jnp.sqrt(scaled_second) + 1e-08) + weight_decay * weight)
    return (weight_new, first_new, second_new)

def block_forward(params, inputs, segment_ids):
    w_qkv, w_out, w_fc, w_proj, vec_norm, vec_split = params
    mat_qkv = low(w_qkv)
    mat_out = low(w_out)
    mat_fc = low(w_fc)
    mat_proj = low(w_proj)
    row_norm = low(vec_norm)
    row_split = low(vec_split)
    blocks, length = segment_ids.shape
    normed_one = low(layer_norm(inputs, row_norm[0], row_norm[1]))
    query_rows = low(low_back(product(normed_one, mat_qkv[0]) + row_split[0]))
    key_rows = low(low_back(product(normed_one, mat_qkv[1])))
    value_rows = low(low_back(product(normed_one, mat_qkv[2]) + row_split[1]))
    query_heads = query_rows.reshape(blocks, length, H, HD)
    key_heads = key_rows.reshape(blocks, length, H, HD)
    value_heads = value_rows.reshape(blocks, length, H, HD)
    scores = low_back(jnp.einsum('bqhd,bkhd->bhqk', query_heads, key_heads, precision=lax.Precision.HIGHEST) * 0.125)
    row_index = lax.broadcasted_iota(jnp.int32, (length, length), 0)
    col_index = lax.broadcasted_iota(jnp.int32, (length, length), 1)
    allowed = (segment_ids[:, :, None] == segment_ids[:, None, :]) & (col_index <= row_index)[None]
    scores = jnp.where(allowed[:, None], scores, -1000000000.0)
    softmax_rows = low(jax.nn.softmax(scores, axis=-1))
    attended = jnp.einsum('bhqk,bkhd->bqhd', softmax_rows, value_heads, precision=lax.Precision.HIGHEST)
    attended = low(low_back(attended.reshape(blocks, length, D)))
    resid = inputs + low_back(product(attended, mat_out)) + row_norm[4]
    normed_two = low(layer_norm(resid, row_norm[2], row_norm[3]))
    hidden_bias = row_split[2:6].T.reshape(-1)
    pre_gate = low_back(product(normed_two, mat_fc) + hidden_bias)
    gate_rows = low(jax.nn.gelu(pre_gate, approximate=True))
    return resid + low_back(product(gate_rows, mat_proj)) + row_norm[5]

def reference(tokens, cotangent, segments, w_qkv, w_out, w_fc, w_proj, vec_norm, vec_split, first_qkv, first_out, first_fc, first_proj, first_norm, first_split, second_qkv, second_out, second_fc, second_proj, second_norm, second_split):
    blocks = MB * N_DP
    group_size = math.gcd(blocks, max(1, 4096 // TOK_MB))
    groups = blocks // group_size
    inputs = tokens.astype(jnp.float32).reshape(groups, group_size, TOK_MB, D)
    upstream = cotangent.astype(jnp.float32).reshape(groups, group_size, TOK_MB, D)
    segment_ids = segments.reshape(groups, group_size, TOK_MB)
    params = (w_qkv, w_out, w_fc, w_proj, vec_norm, vec_split)

    def visit_group(running, group_item):
        group_in, group_up, group_ids = group_item
        group_out, pullback = jax.vjp(lambda weights, values: block_forward(weights, values, group_ids), params, group_in)
        weight_grads, input_grads = pullback(group_up)
        return (jax.tree.map(jnp.add, running, weight_grads), (group_out, input_grads))
    empty_grads = jax.tree.map(jnp.zeros_like, params)
    gradients, (outputs, input_grads) = lax.scan(visit_group, empty_grads, (inputs, upstream, segment_ids))
    out_tokens = outputs.reshape(MB, N_DP * TOK_MB, D).astype(jnp.bfloat16)
    in_grad = input_grads.reshape(MB, N_DP * TOK_MB, D).astype(jnp.bfloat16)
    rates = rate_list()
    decays = (0.1, 0.1, 0.1, 0.1, 0.0, 0.0)
    firsts = (first_qkv, first_out, first_fc, first_proj, first_norm, first_split)
    seconds = (second_qkv, second_out, second_fc, second_proj, second_norm, second_split)
    updated = [adamw(params[index], gradients[index], firsts[index], seconds[index], rates[index], decays[index]) for index in range(6)]
    return (out_tokens, in_grad, updated[0][0], updated[1][0], updated[2][0], updated[3][0], updated[4][0], updated[5][0], updated[0][1], updated[1][1], updated[2][1], updated[3][1], updated[4][1], updated[5][1], updated[0][2], updated[1][2], updated[2][2], updated[3][2], updated[4][2], updated[5][2])
```

```python
import functools
import math

import jax
import jax.numpy as jnp
from jax import lax
from jax.experimental import pallas as pl
from jax.experimental.pallas import tpu as pltpu
from jax.sharding import PartitionSpec as P

D = 1024
HD = 64
FF = 4096
TOK_MB = 64
STEP = 10
BF = jnp.bfloat16
F32 = jnp.float32
EXT = 16
VMEM_LIMIT = 60 * 1024 * 1024

NN = (((1,), (0,)), ((), ()))
NT = (((1,), (1,)), ((), ()))
TN = (((0,), (0,)), ((), ()))


def dot(a, b, dims=NN):
    return lax.dot_general(a, b, dims, preferred_element_type=F32)


def rate_list():
    narrow = D // min(32, max(2, TOK_MB // 4))
    return (
        2.0 / math.sqrt(D),
        2.0 / math.sqrt(narrow),
        2.0 / math.sqrt(D),
        2.0 / math.sqrt(FF),
        0.8,
        0.4,
    )


def adamw(weight, gradient, first_moment, second, step_rate, weight_decay):
    first_new = 0.9 * first_moment + 0.1 * gradient
    second_new = 0.95 * second + 0.05 * gradient * gradient
    scaled_first = first_new / (1.0 - 0.9**STEP)
    scaled_second = second_new / (1.0 - 0.95**STEP)
    weight_new = weight - step_rate * (
        scaled_first / (jnp.sqrt(scaled_second) + 1e-08) + weight_decay * weight
    )
    return (weight_new, first_new, second_new)


def make_parts(widths):
    qkv, out, fc, proj, ext = widths
    half_fc, half_proj = fc // 2, proj // 2
    return (
        (0, 0, qkv, 0),
        (2, half_fc, half_fc, 1),
        (1, 0, out, 0),
        (3, 0, half_proj, 1),
        (2, 0, half_fc, 0),
        (3, half_proj, half_proj, 1),
        (4, 0, ext, 1),
    )


def chip_at(position, chips):
    half = chips // 2
    high = lax.div(position, half)
    return (1 - high) * 2 * position + high * (2 * (chips - 1 - position) + 1)


def position_of(chip, chips):
    odd = lax.rem(chip, 2)
    row = lax.div(chip, 2)
    return (1 - odd) * row + odd * (chips - 1 - row)


def ring_place(chips):
    me = lax.axis_index("dp")
    core = lax.rem(me, 2)
    place = position_of(lax.div(me, 2), chips)

    def device(position):
        return chip_at(lax.rem(position + 2 * chips, chips), chips) * 2 + core

    return me, me + 1 - 2 * core, place, device


def greet(others):
    barrier = pltpu.get_barrier_semaphore()
    for other in others:
        pl.semaphore_signal(
            barrier, inc=1, device_id=other, device_id_type=pl.DeviceIdType.MESH
        )
    pl.semaphore_wait(barrier, len(others))


def remote(src, dst, send, recv, target):
    return pltpu.make_async_remote_copy(
        src_ref=src,
        dst_ref=dst,
        send_sem=send,
        recv_sem=recv,
        device_id={"dp": target},
        device_id_type=pl.DeviceIdType.MESH,
    )


def gather_kernel(chips, parts, *refs):
    ins, outs = refs[:5], refs[5:10]
    ring_send, ring_recv, side_send, side_recv = refs[10:]
    me, sibling, place, device = ring_place(chips)
    neighbours = (device(place + 1), device(place - 1))
    greet([{"dp": neighbours[0]}, {"dp": neighbours[1]}, {"dp": sibling}])
    for index in range(5):
        outs[index][me] = ins[index][...]

    def ring_copy(k, step):
        index, first, wide, way = parts[k]
        owner = device(place - step if way == 0 else place + step)
        block = outs[index].at[owner, :, pl.ds(first, wide)]
        return remote(
            block, block, ring_send.at[k, step], ring_recv.at[k, step], neighbours[way]
        )

    def side_copy(k, step):
        index, first, wide, way = parts[k]
        owner = device(place - step if way == 0 else place + step)
        block = outs[index].at[owner, :, pl.ds(first, wide)]
        return remote(block, block, side_send.at[k, step], side_recv.at[k, step], sibling)

    for k in range(len(parts)):
        ring_copy(k, 0).start()
    for k in range(len(parts)):
        side_copy(k, 0).start()

    @pl.loop(1, chips - 1)
    def _(step):
        for k in range(len(parts)):
            ring_copy(k, step - 1).wait_recv()
            ring_copy(k, step).start()
            side_copy(k, step).start()

    for k in range(len(parts)):
        ring_copy(k, chips - 2).wait_recv()
        side_copy(k, chips - 1).start()

    @pl.loop(0, chips - 1)
    def _(step):
        for k in range(len(parts)):
            ring_copy(k, step).wait_send()

    @pl.loop(0, chips)
    def _(step):
        for k in range(len(parts)):
            side_copy(k, step).wait()


def gather(blocks, count):
    chips = count // 2
    parts = make_parts([block.shape[1] for block in blocks])
    sems = [
        pltpu.SemaphoreType.DMA((len(parts), chips - 1)),
        pltpu.SemaphoreType.DMA((len(parts), chips - 1)),
        pltpu.SemaphoreType.DMA((len(parts), chips)),
        pltpu.SemaphoreType.DMA((len(parts), chips)),
    ]
    return pl.pallas_call(
        functools.partial(gather_kernel, chips, parts),
        out_shape=[jax.ShapeDtypeStruct((count,) + b.shape, b.dtype) for b in blocks],
        in_specs=[pl.BlockSpec(memory_space=pltpu.VMEM)] * 5,
        out_specs=[pl.BlockSpec(memory_space=pltpu.VMEM)] * 5,
        scratch_shapes=sems,
        compiler_params=pltpu.CompilerParams(
            collective_id=0, has_side_effects=True, vmem_limit_bytes=VMEM_LIMIT
        ),
        name="gather_weights",
    )(*blocks)


def reduce_kernel(chips, parts, *refs):
    lhs, rhs, ext = refs[:4], refs[4:8], refs[8]
    outs = refs[9:14]
    bufs = refs[14:19]
    terms = refs[19:24]
    left, right = refs[24:28], refs[28:32]
    ext_other = refs[32]
    ring_send, ring_recv, side_send, side_recv, local_sem = refs[33:]
    tokens = rhs[0].shape[0]
    me, sibling, place, device = ring_place(chips)
    neighbours = (device(place + 1), device(place - 1))
    greet([{"dp": neighbours[0]}, {"dp": neighbours[1]}, {"dp": sibling}])
    sides = []
    locals_ = []
    for m in range(4):
        sides.append(
            remote(
                lhs[m],
                left[m].at[:, :, pl.ds(tokens, tokens)],
                side_send.at[2 * m],
                side_recv.at[2 * m],
                sibling,
            )
        )
        sides.append(
            remote(
                rhs[m],
                right[m].at[pl.ds(tokens, tokens)],
                side_send.at[2 * m + 1],
                side_recv.at[2 * m + 1],
                sibling,
            )
        )
        locals_.append(
            pltpu.make_async_copy(
                lhs[m], left[m].at[:, :, pl.ds(0, tokens)], local_sem.at[2 * m]
            )
        )
        locals_.append(
            pltpu.make_async_copy(
                rhs[m], right[m].at[pl.ds(0, tokens)], local_sem.at[2 * m + 1]
            )
        )
    sides.append(remote(ext, ext_other, side_send.at[8], side_recv.at[8], sibling))
    for copy in sides:
        copy.start()
    for copy in locals_:
        copy.start()
    for copy in sides:
        copy.wait()
    for copy in locals_:
        copy.wait()

    def owner_of(k, step):
        way = parts[k][3]
        return device(place - 1 - step if way == 0 else place + 1 + step)

    def term(k, step):
        index, first, wide, _ = parts[k]
        owner = owner_of(k, step)
        if index == 4:
            return ext[owner] + ext_other[owner]
        return dot(left[index][owner], right[index][:, pl.ds(first, wide)])

    def ring_copy(k, step):
        index, first, wide, way = parts[k]
        columns = pl.ds(first, wide)
        return remote(
            bufs[index].at[step, :, columns],
            bufs[index].at[step + 1, :, columns],
            ring_send.at[k, step],
            ring_recv.at[k, step],
            neighbours[way],
        )

    for k in range(len(parts)):
        index, first, wide, _ = parts[k]
        bufs[index][0, :, pl.ds(first, wide)] = term(k, 0).astype(BF)
        ring_copy(k, 0).start()

    def fill(step):
        for k in range(len(parts)):
            index, first, wide, _ = parts[k]
            terms[index][:, pl.ds(first, wide)] = term(k, step)

    @pl.loop(1, chips - 1)
    def _(step):
        fill(step)
        for k in range(len(parts)):
            index, first, wide, _ = parts[k]
            columns = pl.ds(first, wide)
            ring_copy(k, step - 1).wait_recv()
            bufs[index][step, :, columns] = (
                bufs[index][step, :, columns].astype(F32) + terms[index][:, columns]
            ).astype(BF)
            ring_copy(k, step).start()

    fill(chips - 1)
    for k in range(len(parts)):
        index, first, wide, _ = parts[k]
        columns = pl.ds(first, wide)
        ring_copy(k, chips - 2).wait_recv()
        outs[index][:, columns] = (
            bufs[index][chips - 1, :, columns].astype(F32) + terms[index][:, columns]
        )

    @pl.loop(0, chips - 1)
    def _(step):
        for k in range(len(parts)):
            ring_copy(k, step).wait_send()


def reduce_scatter(lhs, rhs, ext):
    count, rows, tokens = lhs[0].shape
    chips = count // 2
    widths = [r.shape[1] for r in rhs] + [ext.shape[2]]
    heights = [rows] * 4 + [ext.shape[1]]
    parts = make_parts(widths)
    scratch = [pltpu.VMEM((chips, h, w), BF) for h, w in zip(heights, widths)]
    scratch += [pltpu.VMEM((h, w), F32) for h, w in zip(heights, widths)]
    scratch += [pltpu.VMEM((count, rows, 2 * tokens), BF) for _ in range(4)]
    scratch += [pltpu.VMEM((2 * tokens, w), BF) for w in widths[:4]]
    scratch += [pltpu.VMEM(ext.shape, F32)]
    scratch += [
        pltpu.SemaphoreType.DMA((len(parts), chips - 1)),
        pltpu.SemaphoreType.DMA((len(parts), chips - 1)),
        pltpu.SemaphoreType.DMA((9,)),
        pltpu.SemaphoreType.DMA((9,)),
        pltpu.SemaphoreType.DMA((8,)),
    ]
    return pl.pallas_call(
        functools.partial(reduce_kernel, chips, parts),
        out_shape=[jax.ShapeDtypeStruct((h, w), F32) for h, w in zip(heights, widths)],
        in_specs=[pl.BlockSpec(memory_space=pltpu.VMEM)] * 9,
        out_specs=[pl.BlockSpec(memory_space=pltpu.VMEM)] * 5,
        scratch_shapes=scratch,
        compiler_params=pltpu.CompilerParams(
            collective_id=1, has_side_effects=True, vmem_limit_bytes=VMEM_LIMIT
        ),
        name="reduce_gradients",
    )(*lhs, *rhs, ext)


def normalize(values):
    center = values - jnp.mean(values, axis=-1, keepdims=True)
    spread = jnp.mean(center * center, axis=-1, keepdims=True)
    scale = lax.rsqrt(spread + 1e-05)
    return center * scale, scale


def normalize_back(grad, gain, unit, scale):
    inner = grad * gain
    return scale * (
        inner
        - jnp.mean(inner, axis=-1, keepdims=True)
        - unit * jnp.mean(inner * unit, axis=-1, keepdims=True)
    )


def head_mask(shape, which):
    lane = lax.broadcasted_iota(jnp.int32, shape, 1)
    return lax.div(lane, HD) == which


def head_probs(query, key, which, allowed):
    only = jnp.where(head_mask(query.shape, which), query, jnp.zeros_like(query))
    scores = jnp.where(allowed, dot(only, key, NT) * 0.125, -1000000000.0)
    exponent = jnp.exp(scores - jnp.max(scores, axis=-1, keepdims=True))
    return exponent / jnp.sum(exponent, axis=-1, keepdims=True)


def attend_body(tokens, allow, norm, split, w_qkv, w_out, a1, qkv, o, part):
    width = o.shape[1]
    unit, _ = normalize(tokens[...].astype(F32))
    a1[...] = (unit * norm[0:1] + norm[1:2]).astype(BF)
    for t in range(3):
        columns = pl.ds(t * width, width)
        rows = dot(a1[...], w_qkv[:, columns])
        if t != 1:
            rows = rows + split[pl.ds(t // 2, 1)]
        qkv[:, columns] = rows.astype(BF)
    allowed = allow[...] > 0.5
    for pair in range(width // (2 * HD)):
        first = pair * 2 * HD
        query, key, value = (
            qkv[:, pl.ds(t * width + first, 2 * HD)] for t in range(3)
        )
        total = jnp.zeros(query.shape, F32)
        for which in range(2):
            probs = head_probs(query, key, which, allowed).astype(BF)
            only = jnp.where(head_mask(value.shape, which), value, jnp.zeros_like(value))
            total = total + dot(probs, only)
        o[:, pl.ds(first, 2 * HD)] = total.astype(BF)
    part[...] = dot(o[...], w_out[...], NT).astype(BF)


def feed_body(
    tokens, mine, other, cot, norm, bias, w_fc, w_proj, r, a2, gl, dz, part
):
    rows = tokens[...].astype(F32) + (mine[...].astype(F32) + other[...].astype(F32))
    rows = rows + norm[4:5]
    r[...] = rows
    unit, _ = normalize(rows)
    a2[...] = (unit * norm[2:3] + norm[3:4]).astype(BF)
    width = gl.shape[1]
    step = 512
    root = math.sqrt(2.0 / math.pi)
    for first in range(0, width, step):
        columns = pl.ds(first, step)
        z = dot(a2[...], w_fc[:, columns]) + bias[:, columns]
        bent = jnp.tanh(root * (z + 0.044715 * z * z * z))
        gl[:, columns] = (0.5 * z * (1.0 + bent)).astype(BF)
        slope = 0.5 * (1.0 + bent) + 0.5 * z * (1.0 - bent * bent) * root * (
            1.0 + 3.0 * 0.044715 * z * z
        )
        dz[:, columns] = (slope * dot(cot[...], w_proj[:, columns])).astype(BF)
    part[:, pl.ds(0, D)] = dot(gl[...], w_proj[...], NT).astype(BF)
    part[:, pl.ds(D, D)] = dot(dz[...], w_fc[...], NT).astype(BF)


def back_body(
    mine, other, r, cot, allow, norm, qkv, w_out, w_qkv, out, dr, dao, dqkv, part, sums
):
    total = mine[...].astype(F32) + other[...].astype(F32)
    rows = r[...]
    out[...] = (rows + total[:, :D] + norm[5:6]).astype(BF)
    da2 = total[:, D:]
    unit, scale = normalize(rows)
    top = cot[...].astype(F32)
    grad = top + normalize_back(da2, norm[2:3], unit, scale)
    dr[...] = grad
    dao[...] = grad.astype(BF)
    sums[0:1] = jnp.sum(da2 * unit, axis=0, keepdims=True)
    sums[1:2] = jnp.sum(da2, axis=0, keepdims=True)
    sums[2:3] = jnp.sum(grad, axis=0, keepdims=True)
    sums[3:4] = jnp.sum(top, axis=0, keepdims=True)
    sums[4:8] = jnp.zeros((4, D), F32)
    width = w_out.shape[1]
    heads = dot(dao[...], w_out[...]).astype(BF)
    allowed = allow[...] > 0.5
    for pair in range(width // (2 * HD)):
        first = pair * 2 * HD
        query, key, value = (
            qkv[:, pl.ds(t * width + first, 2 * HD)] for t in range(3)
        )
        do = heads[:, first : first + 2 * HD]
        zero = jnp.zeros_like(query)
        dq = jnp.zeros(query.shape, F32)
        dk = jnp.zeros(query.shape, F32)
        dv = jnp.zeros(query.shape, F32)
        for which in range(2):
            mask = head_mask(query.shape, which)
            probs = head_probs(query, key, which, allowed)
            only = jnp.where(mask, do, zero)
            dp = dot(only, value, NT)
            ds = probs * (dp - jnp.sum(probs * dp, axis=-1, keepdims=True))
            ds = ds.astype(BF)
            dq = dq + dot(ds, jnp.where(mask, key, zero))
            dk = dk + dot(ds, jnp.where(mask, query, zero), TN)
            dv = dv + dot(probs.astype(BF), only, TN)
        dqkv[:, pl.ds(first, 2 * HD)] = (dq * 0.125).astype(BF)
        dqkv[:, pl.ds(width + first, 2 * HD)] = (dk * 0.125).astype(BF)
        dqkv[:, pl.ds(2 * width + first, 2 * HD)] = dv.astype(BF)
    part[...] = dot(dqkv[...], w_qkv[...], NT).astype(BF)


def last_body(mine, other, tokens, dr, norm, grad, sums):
    da1 = mine[...].astype(F32) + other[...].astype(F32)
    unit, scale = normalize(tokens[...].astype(F32))
    grad[...] = (dr[...] + normalize_back(da1, norm[0:1], unit, scale)).astype(BF)
    sums[0:1] = jnp.sum(da1 * unit, axis=0, keepdims=True)
    sums[1:2] = jnp.sum(da1, axis=0, keepdims=True)
    sums[2:8] = jnp.zeros((6, D), F32)


def call(body, name, shapes, *args):
    return pl.pallas_call(
        body,
        out_shape=[jax.ShapeDtypeStruct(s, d) for s, d in shapes],
        in_specs=[pl.BlockSpec(memory_space=pltpu.VMEM)] * len(args),
        out_specs=[pl.BlockSpec(memory_space=pltpu.VMEM)] * len(shapes),
        compiler_params=pltpu.CompilerParams(vmem_limit_bytes=VMEM_LIMIT),
        name=name,
    )(*args)


def pack_ext(norm, split):
    rows, columns = norm.shape[1], split.shape[1]

    def wide(values):
        return jnp.pad(values, ((0, 0), (0, 128 - values.shape[1])))

    hidden = split[2:6].T.reshape(1, 4 * columns)
    packed = jnp.concatenate([wide(hidden), wide(norm), wide(split[0:2])], axis=0)
    return jnp.pad(packed, ((0, EXT - packed.shape[0]), (0, 0)))


def local(count, *args):
    (tokens, cotangent, segments, w_qkv, w_out, w_fc, w_proj, vec_norm, vec_split) = args[:9]
    firsts, seconds = args[9:15], args[15:21]
    masters = (w_qkv, w_out, w_fc, w_proj, vec_norm, vec_split)
    rows = w_fc.shape[0]
    width = w_qkv.shape[2]
    hidden = w_fc.shape[1]
    piece = vec_split.shape[1]
    batches, length = tokens.shape[:2]
    total = batches * length
    blocks = (
        w_qkv.transpose(1, 0, 2).reshape(rows, 3 * width).astype(BF),
        w_out.T.astype(BF),
        w_fc.astype(BF),
        w_proj.T.astype(BF),
        pack_ext(vec_norm, vec_split).astype(BF),
    )
    got = gather(blocks, count)
    m_qkv, m_out, m_fc, m_proj = (got[i].reshape(D, got[i].shape[2]) for i in range(4))
    vectors = got[4].astype(F32)
    bias = vectors[:, 0, : 4 * piece].reshape(1, hidden)
    norm = vectors[:, 1:7, :rows].transpose(1, 0, 2).reshape(6, D)
    split = vectors[:, 7:9, :piece].transpose(1, 0, 2).reshape(2, width)
    norm = jnp.pad(norm, ((0, 2), (0, 0)))
    split = jnp.pad(split, ((0, 6), (0, 0)))

    t = tokens.reshape(total, D)
    cot = cotangent.reshape(total, D)
    seg = segments.reshape(total)
    place = jnp.arange(total)
    block = place // length
    allow = (
        (seg[:, None] == seg[None, :])
        & (block[:, None] == block[None, :])
        & (place[None, :] <= place[:, None])
    ).astype(F32)

    def swap(values):
        return lax.ppermute(values, "mp", [(0, 1), (1, 0)])

    a1, qkv, o, part = call(
        attend_body,
        "attend",
        [((total, D), BF), ((total, 3 * width), BF), ((total, width), BF), ((total, D), BF)],
        *(t, allow, norm, split, m_qkv, m_out),
    )
    r, a2, gl, dz, part2 = call(
        feed_body,
        "feed",
        [
            ((total, D), F32),
            ((total, D), BF),
            ((total, hidden), BF),
            ((total, hidden), BF),
            ((total, 2 * D), BF),
        ],
        *(t, part, swap(part), cot, norm, bias, m_fc, m_proj),
    )
    out, dr, dao, dqkv, part3, sums2 = call(
        back_body,
        "back",
        [
            ((total, D), BF),
            ((total, D), F32),
            ((total, D), BF),
            ((total, 3 * width), BF),
            ((total, D), BF),
            ((8, D), F32),
        ],
        *(part2, swap(part2), r, cot, allow, norm, qkv, m_out, m_qkv),
    )
    in_grad, sums1 = call(
        last_body,
        "last",
        [((total, D), BF), ((8, D), F32)],
        *(part3, swap(part3), t, dr, norm),
    )
    norm_sums = jnp.concatenate([sums1[0:2], sums2[0:4]], axis=0)
    stack_sums = jnp.sum(dqkv.astype(F32), axis=0)
    hidden_sums = jnp.sum(dz.astype(F32), axis=0)

    def wide(values):
        return jnp.pad(values, ((0, 0), (0, 0), (0, 128 - values.shape[2])))

    split_sums = jnp.stack([stack_sums[:width], stack_sums[2 * width :]])
    ext = jnp.concatenate(
        [
            wide(hidden_sums.reshape(count, 1, 4 * piece)),
            wide(norm_sums.reshape(6, count, rows).transpose(1, 0, 2)),
            wide(split_sums.reshape(2, count, piece).transpose(1, 0, 2)),
        ],
        axis=1,
    )
    ext = jnp.pad(ext, ((0, 0), (0, EXT - ext.shape[1]), (0, 0)))
    lhs = [v.T.reshape(count, rows, total) for v in (a1, dao, a2, cot)]
    g_qkv, g_out, g_fc, g_proj, g_ext = reduce_scatter(lhs, (dqkv, o, dz, gl), ext)
    reduced = (
        g_qkv.reshape(rows, 3, width).transpose(1, 0, 2),
        g_out.T,
        g_fc,
        g_proj.T,
        g_ext[1:7, :rows],
        jnp.concatenate([g_ext[7:9, :piece], g_ext[0, : 4 * piece].reshape(piece, 4).T]),
    )
    rates = rate_list()
    decays = (0.1, 0.1, 0.1, 0.1, 0.0, 0.0)
    updated = [
        adamw(masters[i], reduced[i], firsts[i], seconds[i], rates[i], decays[i])
        for i in range(6)
    ]
    return (
        out.reshape(tokens.shape),
        in_grad.reshape(tokens.shape),
        *(u[0] for u in updated),
        *(u[1] for u in updated),
        *(u[2] for u in updated),
    )


def solution(mesh):
    shards = (
        P(None, "dp", "mp"),
        P("mp", "dp"),
        P("dp", "mp"),
        P("mp", "dp"),
        P(None, "dp"),
        P(None, ("mp", "dp")),
    )
    rows = P(None, "dp", None)
    return jax.shard_map(
        functools.partial(local, mesh.shape["dp"]),
        mesh=mesh,
        in_specs=(rows, rows, P(None, "dp")) + shards * 3,
        out_specs=(rows, rows) + shards * 3,
        check_vma=False,
    )
```

```python
import functools
import math

import jax
import jax.numpy as jnp
from jax import lax
from jax.experimental import pallas as pl
from jax.experimental.pallas import tpu as pltpu
from jax.sharding import PartitionSpec as P

D = 1024
HD = 64
FF = 4096
TOK_MB = 64
STEP = 10
BF = jnp.bfloat16
F32 = jnp.float32
EXT = 16
VMEM_LIMIT = 60 * 1024 * 1024

NN = (((1,), (0,)), ((), ()))
NT = (((1,), (1,)), ((), ()))
TN = (((0,), (0,)), ((), ()))


def dot(a, b, dims=NN):
    return lax.dot_general(a, b, dims, preferred_element_type=F32)


def rate_list():
    narrow = D // min(32, max(2, TOK_MB // 4))
    return (
        2.0 / math.sqrt(D),
        2.0 / math.sqrt(narrow),
        2.0 / math.sqrt(D),
        2.0 / math.sqrt(FF),
        0.8,
        0.4,
    )


def adamw(weight, gradient, first_moment, second, step_rate, weight_decay):
    first_new = 0.9 * first_moment + 0.1 * gradient
    second_new = 0.95 * second + 0.05 * gradient * gradient
    scaled_first = first_new / (1.0 - 0.9**STEP)
    scaled_second = second_new / (1.0 - 0.95**STEP)
    weight_new = weight - step_rate * (
        scaled_first / (jnp.sqrt(scaled_second) + 1e-08) + weight_decay * weight
    )
    return (weight_new, first_new, second_new)


def make_parts(widths):
    qkv, out, fc, proj, ext = widths
    half_fc, half_proj = fc // 2, proj // 2
    return (
        (0, 0, qkv, 0),
        (2, half_fc, half_fc, 1),
        (1, 0, out, 0),
        (3, 0, half_proj, 1),
        (2, 0, half_fc, 0),
        (3, half_proj, half_proj, 1),
        (4, 0, ext, 1),
    )


def chip_at(position, chips):
    half = chips // 2
    high = lax.div(position, half)
    return (1 - high) * 2 * position + high * (2 * (chips - 1 - position) + 1)


def position_of(chip, chips):
    odd = lax.rem(chip, 2)
    row = lax.div(chip, 2)
    return (1 - odd) * row + odd * (chips - 1 - row)


def ring_place(chips):
    me = lax.axis_index("dp")
    core = lax.rem(me, 2)
    place = position_of(lax.div(me, 2), chips)

    def device(position):
        return chip_at(lax.rem(position + 2 * chips, chips), chips) * 2 + core

    return me, me + 1 - 2 * core, place, device


def greet(others):
    barrier = pltpu.get_barrier_semaphore()
    for other in others:
        pl.semaphore_signal(
            barrier, inc=1, device_id=other, device_id_type=pl.DeviceIdType.MESH
        )
    pl.semaphore_wait(barrier, len(others))


def remote(src, dst, send, recv, target):
    return pltpu.make_async_remote_copy(
        src_ref=src,
        dst_ref=dst,
        send_sem=send,
        recv_sem=recv,
        device_id={"dp": target},
        device_id_type=pl.DeviceIdType.MESH,
    )


def gather_kernel(chips, parts, *refs):
    ins, outs = refs[:5], refs[5:10]
    ring_send, ring_recv, side_send, side_recv = refs[10:]
    me, sibling, place, device = ring_place(chips)
    neighbours = (device(place + 1), device(place - 1))
    greet([{"dp": neighbours[0]}, {"dp": neighbours[1]}, {"dp": sibling}])
    for index in range(5):
        outs[index][me] = ins[index][...]

    def ring_copy(k, step):
        index, first, wide, way = parts[k]
        owner = device(place - step if way == 0 else place + step)
        block = outs[index].at[owner, :, pl.ds(first, wide)]
        return remote(
            block, block, ring_send.at[k, step], ring_recv.at[k, step], neighbours[way]
        )

    def side_copy(k, step):
        index, first, wide, way = parts[k]
        owner = device(place - step if way == 0 else place + step)
        block = outs[index].at[owner, :, pl.ds(first, wide)]
        return remote(block, block, side_send.at[k, step], side_recv.at[k, step], sibling)

    for k in range(len(parts)):
        ring_copy(k, 0).start()
    for k in range(len(parts)):
        side_copy(k, 0).start()

    @pl.loop(1, chips - 1)
    def _(step):
        for k in range(len(parts)):
            ring_copy(k, step - 1).wait_recv()
            ring_copy(k, step).start()
            side_copy(k, step).start()

    for k in range(len(parts)):
        ring_copy(k, chips - 2).wait_recv()
        side_copy(k, chips - 1).start()

    @pl.loop(0, chips - 1)
    def _(step):
        for k in range(len(parts)):
            ring_copy(k, step).wait_send()

    @pl.loop(0, chips)
    def _(step):
        for k in range(len(parts)):
            side_copy(k, step).wait()


def gather(blocks, count):
    chips = count // 2
    parts = make_parts([block.shape[1] for block in blocks])
    sems = [
        pltpu.SemaphoreType.DMA((len(parts), chips - 1)),
        pltpu.SemaphoreType.DMA((len(parts), chips - 1)),
        pltpu.SemaphoreType.DMA((len(parts), chips)),
        pltpu.SemaphoreType.DMA((len(parts), chips)),
    ]
    return pl.pallas_call(
        functools.partial(gather_kernel, chips, parts),
        out_shape=[jax.ShapeDtypeStruct((count,) + b.shape, b.dtype) for b in blocks],
        in_specs=[pl.BlockSpec(memory_space=pltpu.VMEM)] * 5,
        out_specs=[pl.BlockSpec(memory_space=pltpu.VMEM)] * 5,
        scratch_shapes=sems,
        compiler_params=pltpu.CompilerParams(
            collective_id=0, has_side_effects=True, vmem_limit_bytes=VMEM_LIMIT
        ),
        name="gather_weights",
    )(*blocks)


def reduce_kernel(chips, parts, *refs):
    lhs, rhs, ext = refs[:4], refs[4:8], refs[8]
    outs = refs[9:14]
    bufs = refs[14:19]
    terms = refs[19:24]
    left, right = refs[24:28], refs[28:32]
    ext_other = refs[32]
    ring_send, ring_recv, side_send, side_recv, local_sem = refs[33:]
    tokens = rhs[0].shape[0]
    me, sibling, place, device = ring_place(chips)
    neighbours = (device(place + 1), device(place - 1))
    greet([{"dp": neighbours[0]}, {"dp": neighbours[1]}, {"dp": sibling}])
    sides = []
    locals_ = []
    for m in range(4):
        sides.append(
            remote(
                lhs[m],
                left[m].at[:, :, pl.ds(tokens, tokens)],
                side_send.at[2 * m],
                side_recv.at[2 * m],
                sibling,
            )
        )
        sides.append(
            remote(
                rhs[m],
                right[m].at[pl.ds(tokens, tokens)],
                side_send.at[2 * m + 1],
                side_recv.at[2 * m + 1],
                sibling,
            )
        )
        locals_.append(
            pltpu.make_async_copy(
                lhs[m], left[m].at[:, :, pl.ds(0, tokens)], local_sem.at[2 * m]
            )
        )
        locals_.append(
            pltpu.make_async_copy(
                rhs[m], right[m].at[pl.ds(0, tokens)], local_sem.at[2 * m + 1]
            )
        )
    sides.append(remote(ext, ext_other, side_send.at[8], side_recv.at[8], sibling))
    for copy in sides:
        copy.start()
    for copy in locals_:
        copy.start()
    for copy in sides:
        copy.wait()
    for copy in locals_:
        copy.wait()

    def owner_of(k, step):
        way = parts[k][3]
        return device(place - 1 - step if way == 0 else place + 1 + step)

    def term(k, step):
        index, first, wide, _ = parts[k]
        owner = owner_of(k, step)
        if index == 4:
            return ext[owner] + ext_other[owner]
        return dot(left[index][owner], right[index][:, pl.ds(first, wide)])

    def ring_copy(k, step):
        index, first, wide, way = parts[k]
        columns = pl.ds(first, wide)
        return remote(
            bufs[index].at[step, :, columns],
            bufs[index].at[step + 1, :, columns],
            ring_send.at[k, step],
            ring_recv.at[k, step],
            neighbours[way],
        )

    for k in range(len(parts)):
        index, first, wide, _ = parts[k]
        bufs[index][0, :, pl.ds(first, wide)] = term(k, 0).astype(BF)
        ring_copy(k, 0).start()

    def fill(step):
        for k in range(len(parts)):
            index, first, wide, _ = parts[k]
            terms[index][:, pl.ds(first, wide)] = term(k, step)

    @pl.loop(1, chips - 1)
    def _(step):
        fill(step)
        for k in range(len(parts)):
            index, first, wide, _ = parts[k]
            columns = pl.ds(first, wide)
            ring_copy(k, step - 1).wait_recv()
            bufs[index][step, :, columns] = (
                bufs[index][step, :, columns].astype(F32) + terms[index][:, columns]
            ).astype(BF)
            ring_copy(k, step).start()

    fill(chips - 1)
    for k in range(len(parts)):
        index, first, wide, _ = parts[k]
        columns = pl.ds(first, wide)
        ring_copy(k, chips - 2).wait_recv()
        outs[index][:, columns] = (
            bufs[index][chips - 1, :, columns].astype(F32) + terms[index][:, columns]
        )

    @pl.loop(0, chips - 1)
    def _(step):
        for k in range(len(parts)):
            ring_copy(k, step).wait_send()


def reduce_scatter(lhs, rhs, ext):
    count, rows, tokens = lhs[0].shape
    chips = count // 2
    widths = [r.shape[1] for r in rhs] + [ext.shape[2]]
    heights = [rows] * 4 + [ext.shape[1]]
    parts = make_parts(widths)
    scratch = [pltpu.VMEM((chips, h, w), BF) for h, w in zip(heights, widths)]
    scratch += [pltpu.VMEM((h, w), F32) for h, w in zip(heights, widths)]
    scratch += [pltpu.VMEM((count, rows, 2 * tokens), BF) for _ in range(4)]
    scratch += [pltpu.VMEM((2 * tokens, w), BF) for w in widths[:4]]
    scratch += [pltpu.VMEM(ext.shape, F32)]
    scratch += [
        pltpu.SemaphoreType.DMA((len(parts), chips - 1)),
        pltpu.SemaphoreType.DMA((len(parts), chips - 1)),
        pltpu.SemaphoreType.DMA((9,)),
        pltpu.SemaphoreType.DMA((9,)),
        pltpu.SemaphoreType.DMA((8,)),
    ]
    return pl.pallas_call(
        functools.partial(reduce_kernel, chips, parts),
        out_shape=[jax.ShapeDtypeStruct((h, w), F32) for h, w in zip(heights, widths)],
        in_specs=[pl.BlockSpec(memory_space=pltpu.VMEM)] * 9,
        out_specs=[pl.BlockSpec(memory_space=pltpu.VMEM)] * 5,
        scratch_shapes=scratch,
        compiler_params=pltpu.CompilerParams(
            collective_id=1, has_side_effects=True, vmem_limit_bytes=VMEM_LIMIT
        ),
        name="reduce_gradients",
    )(*lhs, *rhs, ext)


def normalize(values):
    center = values - jnp.mean(values, axis=-1, keepdims=True)
    spread = jnp.mean(center * center, axis=-1, keepdims=True)
    scale = lax.rsqrt(spread + 1e-05)
    return center * scale, scale


def normalize_back(grad, gain, unit, scale):
    inner = grad * gain
    return scale * (
        inner
        - jnp.mean(inner, axis=-1, keepdims=True)
        - unit * jnp.mean(inner * unit, axis=-1, keepdims=True)
    )


def head_mask(shape, which):
    lane = lax.broadcasted_iota(jnp.int32, shape, 1)
    return lax.div(lane, HD) == which


def head_probs(query, key, which, allowed):
    only = jnp.where(head_mask(query.shape, which), query, jnp.zeros_like(query))
    scores = jnp.where(allowed, dot(only, key, NT) * 0.125, -1000000000.0)
    exponent = jnp.exp(scores - jnp.max(scores, axis=-1, keepdims=True))
    return exponent / jnp.sum(exponent, axis=-1, keepdims=True)


def attend_body(tokens, allow, norm, split, w_qkv, w_out, a1, qkv, o, part):
    width = o.shape[1]
    unit, _ = normalize(tokens[...].astype(F32))
    a1[...] = (unit * norm[0:1] + norm[1:2]).astype(BF)
    for t in range(3):
        columns = pl.ds(t * width, width)
        rows = dot(a1[...], w_qkv[:, columns])
        if t != 1:
            rows = rows + split[pl.ds(t // 2, 1)]
        qkv[:, columns] = rows.astype(BF)
    allowed = allow[...] > 0.5
    for pair in range(width // (2 * HD)):
        first = pair * 2 * HD
        query, key, value = (
            qkv[:, pl.ds(t * width + first, 2 * HD)] for t in range(3)
        )
        total = jnp.zeros(query.shape, F32)
        for which in range(2):
            probs = head_probs(query, key, which, allowed).astype(BF)
            only = jnp.where(head_mask(value.shape, which), value, jnp.zeros_like(value))
            total = total + dot(probs, only)
        o[:, pl.ds(first, 2 * HD)] = total.astype(BF)
    part[...] = dot(o[...], w_out[...], NT).astype(BF)


def feed_body(
    tokens, mine, other, cot, norm, bias, w_fc, w_proj, r, a2, gl, dz, part
):
    rows = tokens[...].astype(F32) + (mine[...].astype(F32) + other[...].astype(F32))
    rows = rows + norm[4:5]
    r[...] = rows
    unit, _ = normalize(rows)
    a2[...] = (unit * norm[2:3] + norm[3:4]).astype(BF)
    width = gl.shape[1]
    step = 512
    root = math.sqrt(2.0 / math.pi)
    for first in range(0, width, step):
        columns = pl.ds(first, step)
        z = dot(a2[...], w_fc[:, columns]) + bias[:, columns]
        bent = jnp.tanh(root * (z + 0.044715 * z * z * z))
        gl[:, columns] = (0.5 * z * (1.0 + bent)).astype(BF)
        slope = 0.5 * (1.0 + bent) + 0.5 * z * (1.0 - bent * bent) * root * (
            1.0 + 3.0 * 0.044715 * z * z
        )
        dz[:, columns] = (slope * dot(cot[...], w_proj[:, columns])).astype(BF)
    part[:, pl.ds(0, D)] = dot(gl[...], w_proj[...], NT).astype(BF)
    part[:, pl.ds(D, D)] = dot(dz[...], w_fc[...], NT).astype(BF)


def back_body(
    mine, other, r, cot, allow, norm, qkv, w_out, w_qkv, out, dr, dao, dqkv, part, sums
):
    total = mine[...].astype(F32) + other[...].astype(F32)
    rows = r[...]
    out[...] = (rows + total[:, :D] + norm[5:6]).astype(BF)
    da2 = total[:, D:]
    unit, scale = normalize(rows)
    top = cot[...].astype(F32)
    grad = top + normalize_back(da2, norm[2:3], unit, scale)
    dr[...] = grad
    dao[...] = grad.astype(BF)
    sums[0:1] = jnp.sum(da2 * unit, axis=0, keepdims=True)
    sums[1:2] = jnp.sum(da2, axis=0, keepdims=True)
    sums[2:3] = jnp.sum(grad, axis=0, keepdims=True)
    sums[3:4] = jnp.sum(top, axis=0, keepdims=True)
    sums[4:8] = jnp.zeros((4, D), F32)
    width = w_out.shape[1]
    heads = dot(dao[...], w_out[...]).astype(BF)
    allowed = allow[...] > 0.5
    for pair in range(width // (2 * HD)):
        first = pair * 2 * HD
        query, key, value = (
            qkv[:, pl.ds(t * width + first, 2 * HD)] for t in range(3)
        )
        do = heads[:, first : first + 2 * HD]
        zero = jnp.zeros_like(query)
        dq = jnp.zeros(query.shape, F32)
        dk = jnp.zeros(query.shape, F32)
        dv = jnp.zeros(query.shape, F32)
        for which in range(2):
            mask = head_mask(query.shape, which)
            probs = head_probs(query, key, which, allowed)
            only = jnp.where(mask, do, zero)
            dp = dot(only, value, NT)
            ds = probs * (dp - jnp.sum(probs * dp, axis=-1, keepdims=True))
            ds = ds.astype(BF)
            dq = dq + dot(ds, jnp.where(mask, key, zero))
            dk = dk + dot(ds, jnp.where(mask, query, zero), TN)
            dv = dv + dot(probs.astype(BF), only, TN)
        dqkv[:, pl.ds(first, 2 * HD)] = (dq * 0.125).astype(BF)
        dqkv[:, pl.ds(width + first, 2 * HD)] = (dk * 0.125).astype(BF)
        dqkv[:, pl.ds(2 * width + first, 2 * HD)] = dv.astype(BF)
    part[...] = dot(dqkv[...], w_qkv[...], NT).astype(BF)


def last_body(mine, other, tokens, dr, norm, grad, sums):
    da1 = mine[...].astype(F32) + other[...].astype(F32)
    unit, scale = normalize(tokens[...].astype(F32))
    grad[...] = (dr[...] + normalize_back(da1, norm[0:1], unit, scale)).astype(BF)
    sums[0:1] = jnp.sum(da1 * unit, axis=0, keepdims=True)
    sums[1:2] = jnp.sum(da1, axis=0, keepdims=True)
    sums[2:8] = jnp.zeros((6, D), F32)


def call(body, name, shapes, *args):
    return pl.pallas_call(
        body,
        out_shape=[jax.ShapeDtypeStruct(s, d) for s, d in shapes],
        in_specs=[pl.BlockSpec(memory_space=pltpu.VMEM)] * len(args),
        out_specs=[pl.BlockSpec(memory_space=pltpu.VMEM)] * len(shapes),
        compiler_params=pltpu.CompilerParams(vmem_limit_bytes=VMEM_LIMIT),
        name=name,
    )(*args)


def pack_ext(norm, split):
    rows, columns = norm.shape[1], split.shape[1]

    def wide(values):
        return jnp.pad(values, ((0, 0), (0, 128 - values.shape[1])))

    hidden = split[2:6].T.reshape(1, 4 * columns)
    packed = jnp.concatenate([wide(hidden), wide(norm), wide(split[0:2])], axis=0)
    return jnp.pad(packed, ((0, EXT - packed.shape[0]), (0, 0)))


def mega_kernel(chips, *refs):
    (tokens, cot, allow, i_qkv, i_out, i_fc, i_proj, i_ext) = refs[:8]
    out, grad = refs[8:10]
    outs = refs[10:15]
    full = refs[15:20]
    bufs = refs[20:25]
    terms = refs[25:30]
    left, right = refs[30:34], refs[34:38]
    (norm, split, bias, qkv, r, a2, slope, dr, ext, ext_other) = refs[38:48]
    mine, other = refs[48:51], refs[51:54]
    (g_send, g_recv, gs_send, gs_recv, r_send, r_recv, s_send, s_recv, m_send, m_recv) = refs[54:]

    count = 2 * chips
    rows = i_fc.shape[0]
    total = tokens.shape[0]
    width = i_out.shape[0]
    hidden = i_fc.shape[1]
    me, sibling, place, device = ring_place(chips)
    peer = 1 - lax.axis_index("mp")
    neighbours = (device(place + 1), device(place - 1))
    greet(
        [{"dp": neighbours[0]}, {"dp": neighbours[1]}, {"dp": sibling}, {"mp": peer}]
    )

    h_qkv, h_out, q_ff = 3 * width // 2, width // 2, hidden // 4
    groups = (
        [(4, 0, 128, 0), (0, 0, h_qkv, 0), (0, h_qkv, h_qkv, 1)]
        + [(1, 0, h_out, 0), (1, h_out, h_out, 1)],
        [(2, j * q_ff, q_ff, j % 2) for j in range(4)],
        [(3, j * q_ff, q_ff, j % 2) for j in range(4)],
    )
    parts, members = [], []
    for group in groups:
        members.append(list(range(len(parts), len(parts) + len(group))))
        parts += group

    def rows_of(index, owner):
        high = EXT if index == 4 else rows
        return pl.ds(pl.multiple_of(owner * high, high), high)

    def block(k, step):
        index, first, wide, way = parts[k]
        owner = device(place - step if way == 0 else place + step)
        return full[index].at[rows_of(index, owner), pl.ds(first, wide)]

    def ring_copy(k, step):
        ref = block(k, step)
        return remote(ref, ref, g_send.at[k, step], g_recv.at[k, step], neighbours[parts[k][3]])

    def side_copy(k, step):
        ref = block(k, step)
        return remote(ref, ref, gs_send.at[k, step], gs_recv.at[k, step], sibling)

    def gather_step(group, step):
        for k in members[group]:
            if step > 0:
                ring_copy(k, step - 1).wait_recv()
            if step < chips - 1:
                ring_copy(k, step).start()
            side_copy(k, step).start()

    def gather_end(group):
        for k in members[group]:
            for step in range(chips):
                side_copy(k, step).wait_recv()

    def to_side(m):
        pairs = (
            (left[m].at[:, pl.ds(0, total)], left[m].at[:, pl.ds(total, total)]),
            (right[m].at[pl.ds(0, total)], right[m].at[pl.ds(total, total)]),
        )
        return [
            remote(src, dst, s_send.at[2 * m + j], s_recv.at[2 * m + j], sibling)
            for j, (src, dst) in enumerate(pairs)
        ]

    side_ext = remote(ext, ext_other, s_send.at[8], s_recv.at[8], sibling)

    def to_peer(j):
        return pltpu.make_async_remote_copy(
            src_ref=mine[j],
            dst_ref=other[j],
            send_sem=m_send.at[j],
            recv_sem=m_recv.at[j],
            device_id={"mp": peer},
            device_id_type=pl.DeviceIdType.MESH,
        )

    def flip(values):
        return values.astype(F32).T.astype(BF)

    def reduce_rows(index, k, step):
        way = parts[k][3]
        owner = device(place - 1 - step if way == 0 else place + 1 + step)
        return rows_of(index, owner)

    def term(k, step):
        index, first, wide, _ = parts[k]
        at = reduce_rows(index, k, step)
        if index == 4:
            return ext[at, :] + ext_other[at, :]
        return dot(left[index][at, :], right[index][:, pl.ds(first, wide)])

    def sum_copy(k, step):
        index, first, wide, way = parts[k]
        columns = pl.ds(first, wide)
        return remote(
            bufs[index].at[step, :, columns],
            bufs[index].at[step + 1, :, columns],
            r_send.at[k, step],
            r_recv.at[k, step],
            neighbours[way],
        )

    def reduce_step(ks, step):
        if step == 0:
            for k in ks:
                index, first, wide, _ = parts[k]
                bufs[index][0, :, pl.ds(first, wide)] = term(k, 0).astype(BF)
                sum_copy(k, 0).start()
            return
        for k in ks:
            index, first, wide, _ = parts[k]
            terms[index][:, pl.ds(first, wide)] = term(k, step)
        for k in ks:
            index, first, wide, _ = parts[k]
            columns = pl.ds(first, wide)
            sum_copy(k, step - 1).wait_recv()
            value = bufs[index][step, :, columns].astype(F32) + terms[index][:, columns]
            if step < chips - 1:
                bufs[index][step, :, columns] = value.astype(BF)
                sum_copy(k, step).start()
            else:
                outs[index][:, columns] = value

    own = rows_of(0, me)
    full[4][rows_of(4, me), :] = i_ext[...].astype(BF)
    for t in range(3):
        full[0][own, pl.ds(t * width, width)] = i_qkv[t].astype(BF)
    full[1][own, :] = i_out[...].T.astype(BF)
    gather_step(0, 0)
    full[2][own, :] = i_fc[...].astype(BF)
    full[3][own, :] = i_proj[...].T.astype(BF)
    left[3][:, pl.ds(0, total)] = flip(cot[...])
    here = pl.ds(0, total)

    def vectors():
        for j in range(count):
            bias[:, pl.ds(j * 128, 128)] = full[4][pl.ds(j * EXT, EXT), :].astype(F32)
        each = 128 // rows
        for j in range(count // each):
            norm[:, pl.ds(j * 128, 128)] = sum(
                full[4][pl.ds((j * each + i) * EXT, EXT), :].astype(F32) for i in range(each)
            )
        each = count * 128 // width
        for j in range(count // each):
            split[:, pl.ds(j * 128, 128)] = sum(
                full[4][pl.ds((j * each + i) * EXT, EXT), :].astype(F32) for i in range(each)
            )

    def first_norm():
        vectors()
        unit, _ = normalize(tokens[...].astype(F32))
        mine[0][...] = (unit * norm[1:2] + norm[2:3]).astype(BF)
        left[0][:, here] = flip(mine[0][...])

    def project(t):
        columns = pl.ds(t * width, width)
        values = dot(mine[0][...], full[0][:, columns])
        if t != 1:
            values = values + split[pl.ds(7 + t // 2, 1)]
        qkv[:, columns] = values.astype(BF)

    def heads_of(pair):
        first = pair * 2 * HD
        return [qkv[:, pl.ds(t * width + first, 2 * HD)] for t in range(3)]

    def attend(pair):
        query, key, value = heads_of(pair)
        allowed = allow[...] > 0.5
        result = jnp.zeros(query.shape, F32)
        for which in range(2):
            probs = head_probs(query, key, which, allowed).astype(BF)
            only = jnp.where(head_mask(value.shape, which), value, jnp.zeros_like(value))
            result = result + dot(probs, only)
        right[1][here, pl.ds(pair * 2 * HD, 2 * HD)] = result.astype(BF)

    def attend_out():
        mine[0][...] = dot(right[1][here, :], full[1][...], NT).astype(BF)
        to_peer(0).start()

    def second_norm():
        to_peer(0).wait()
        values = tokens[...].astype(F32) + (mine[0][...].astype(F32) + other[0][...].astype(F32))
        values = values + norm[5:6]
        r[...] = values
        unit, _ = normalize(values)
        a2[...] = (unit * norm[3:4] + norm[4:5]).astype(BF)
        left[2][:, here] = flip(a2[...])

    root = math.sqrt(2.0 / math.pi)

    def gelu(j):
        columns = pl.ds(j * q_ff, q_ff)
        z = dot(a2[...], full[2][:, columns]) + bias[0:1, columns]
        bent = jnp.tanh(root * (z + 0.044715 * z * z * z))
        right[3][here, columns] = (0.5 * z * (1.0 + bent)).astype(BF)
        slope[:, columns] = 0.5 * (1.0 + bent) + 0.5 * z * (1.0 - bent * bent) * root * (
            1.0 + 3.0 * 0.044715 * z * z
        )

    def start_all(copies):
        for copy in copies:
            copy.start()

    def wait_all(copies):
        for copy in copies:
            copy.wait()

    pairs = width // (2 * HD)
    lag = chips // 2
    units = [
        [lambda: gather_end(0), first_norm, lambda: project(0)],
        [lambda: project(1), lambda: project(2)],
        [lambda j=j: attend(j) for j in range(pairs)],
        [attend_out],
        [lambda: gather_end(1)],
        [second_norm],
        [lambda: gelu(0), lambda: gelu(1)],
        [lambda: gelu(2), lambda: gelu(3), lambda: start_all(to_side(3))],
    ]
    for tick in range(2 * lag + chips):
        for group in range(3):
            step = tick - lag * group
            if 0 <= step < chips and (group, step) != (0, 0):
                gather_step(group, step)
        if tick >= chips:
            for unit in units[tick - chips]:
                unit()
    gather_end(2)

    def gate_back(j):
        columns = pl.ds(j * q_ff, q_ff)
        right[2][here, columns] = (
            slope[:, columns] * dot(cot[...], full[3][:, columns])
        ).astype(BF)

    def feed_out():
        mine[1][:, pl.ds(0, D)] = dot(right[3][here, :], full[3][...], NT).astype(BF)

    def feed_back():
        mine[1][:, pl.ds(D, D)] = dot(right[2][here, :], full[2][...], NT).astype(BF)
        to_peer(1).start()

    def second_back():
        to_peer(1).wait()
        out[...] = (
            r[...]
            + (mine[1][:, pl.ds(0, D)].astype(F32) + other[1][:, pl.ds(0, D)].astype(F32))
            + norm[6:7]
        ).astype(BF)
        da2 = mine[1][:, pl.ds(D, D)].astype(F32) + other[1][:, pl.ds(D, D)].astype(F32)
        unit, scale = normalize(r[...])
        top = cot[...].astype(F32)
        value = top + normalize_back(da2, norm[3:4], unit, scale)
        dr[...] = value
        a2[...] = value.astype(BF)
        left[1][:, here] = flip(a2[...])
        sums = [da2 * unit, da2, value, top]
        for j in range(4):
            line = jnp.sum(sums[j], axis=0, keepdims=True)
            for d in range(count):
                ext[pl.ds(d * EXT + 3 + j, 1), :] = line[:, d * rows // 128 * 128 :][:, :128]

    def heads_back():
        r[:, pl.ds(0, width)] = dot(a2[...], full[1][...])

    def attend_back(pair):
        query, key, value = heads_of(pair)
        first = pair * 2 * HD
        do = r[:, pl.ds(first, 2 * HD)].astype(BF)
        allowed = allow[...] > 0.5
        zero = jnp.zeros_like(query)
        dq = jnp.zeros(query.shape, F32)
        dk = jnp.zeros(query.shape, F32)
        dv = jnp.zeros(query.shape, F32)
        for which in range(2):
            mask = head_mask(query.shape, which)
            probs = head_probs(query, key, which, allowed)
            only = jnp.where(mask, do, zero)
            dp = dot(only, value, NT)
            ds = probs * (dp - jnp.sum(probs * dp, axis=-1, keepdims=True))
            ds = ds.astype(BF)
            dq = dq + dot(ds, jnp.where(mask, key, zero))
            dk = dk + dot(ds, jnp.where(mask, query, zero), TN)
            dv = dv + dot(probs.astype(BF), only, TN)
        right[0][here, pl.ds(first, 2 * HD)] = (dq * 0.125).astype(BF)
        right[0][here, pl.ds(width + first, 2 * HD)] = (dk * 0.125).astype(BF)
        right[0][here, pl.ds(2 * width + first, 2 * HD)] = dv.astype(BF)

    def attend_in():
        mine[2][...] = dot(right[0][here, :], full[0][...], NT).astype(BF)
        to_peer(2).start()

    def first_back():
        to_peer(2).wait()
        da1 = mine[2][...].astype(F32) + other[2][...].astype(F32)
        unit, scale = normalize(tokens[...].astype(F32))
        grad[...] = (dr[...] + normalize_back(da1, norm[1:2], unit, scale)).astype(BF)
        lines = [jnp.sum(da1 * unit, axis=0, keepdims=True), jnp.sum(da1, axis=0, keepdims=True)]
        heads = jnp.sum(right[0][here, :].astype(F32), axis=0, keepdims=True)
        gates = jnp.sum(right[2][here, :].astype(F32), axis=0, keepdims=True)
        each = count * 128 // width
        for d in range(count):
            ext[pl.ds(d * EXT, 1), :] = gates[:, d * 128 : (d + 1) * 128]
            for j in range(2):
                ext[pl.ds(d * EXT + 1 + j, 1), :] = lines[j][:, d * rows // 128 * 128 :][:, :128]
                at = 2 * j * width + d // each * 128
                ext[pl.ds(d * EXT + 7 + j, 1), :] = heads[:, at : at + 128]
        side_ext.start()

    ext[...] = jnp.zeros(ext.shape, F32)
    waves = (
        (members[2], 0, lambda: wait_all(to_side(3))),
        (members[1], 3, lambda: wait_all(to_side(2))),
        (members[0][1:], 8, lambda: wait_all(to_side(0) + to_side(1))),
        (members[0][:1], 9, side_ext.wait),
    )
    units = [
        [lambda: gate_back(0), lambda: gate_back(1), lambda: gate_back(2)]
        + [lambda: gate_back(3), lambda: start_all(to_side(2))],
        [feed_back, feed_out],
        [],
        [],
        [second_back, lambda: start_all(to_side(1))],
        [heads_back] + [lambda j=j: attend_back(j) for j in range(pairs // 2)],
        [lambda j=j: attend_back(j) for j in range(pairs // 2, pairs)]
        + [lambda: start_all(to_side(0))],
        [attend_in],
        [first_back],
    ]
    units[1] = [feed_out, feed_back]
    for tick in range(9 + chips):
        for ks, begin, ready in waves:
            step = tick - begin
            if step == 0:
                ready()
            if 0 <= step < chips:
                reduce_step(ks, step)
        if tick < len(units):
            for unit in units[tick]:
                unit()

    for k in range(len(parts)):
        for step in range(chips - 1):
            ring_copy(k, step).wait_send()
            sum_copy(k, step).wait_send()
        for step in range(chips):
            side_copy(k, step).wait_send()


def mega(count, tokens, cot, allow, w_qkv, w_out, w_fc, w_proj, ext):
    chips = count // 2
    total = tokens.shape[0]
    rows, hidden = w_fc.shape
    width = w_out.shape[0]
    widths = (3 * width, width, hidden, hidden, 128)
    heights = (rows, rows, rows, rows, EXT)
    scratch = [pltpu.VMEM((count * h, w), BF) for h, w in zip(heights, widths)]
    scratch += [pltpu.VMEM((chips, h, w), BF) for h, w in zip(heights, widths)]
    scratch += [pltpu.VMEM((h, w), F32) for h, w in zip(heights, widths)]
    scratch += [pltpu.VMEM((D, 2 * total), BF) for _ in range(4)]
    scratch += [pltpu.VMEM((2 * total, w), BF) for w in widths[:4]]
    scratch += [
        pltpu.VMEM((EXT, D), F32),
        pltpu.VMEM((EXT, width), F32),
        pltpu.VMEM((EXT, hidden), F32),
        pltpu.VMEM((total, 3 * width), BF),
        pltpu.VMEM((total, D), F32),
        pltpu.VMEM((total, D), BF),
        pltpu.VMEM((total, hidden), F32),
        pltpu.VMEM((total, D), F32),
        pltpu.VMEM((count * EXT, 128), F32),
        pltpu.VMEM((count * EXT, 128), F32),
    ]
    scratch += [pltpu.VMEM((total, w), BF) for w in (D, 2 * D, D)] * 2
    n_parts = 13
    sem = pltpu.SemaphoreType.DMA
    scratch += [sem((n_parts, chips - 1))] * 2 + [sem((n_parts, chips))] * 2
    scratch += [sem((n_parts, chips - 1))] * 2 + [sem((9,))] * 2 + [sem((3,))] * 2
    shapes = [((total, D), BF)] * 2 + [((h, w), F32) for h, w in zip(heights, widths)]
    return pl.pallas_call(
        functools.partial(mega_kernel, chips),
        out_shape=[jax.ShapeDtypeStruct(s, d) for s, d in shapes],
        in_specs=[pl.BlockSpec(memory_space=pltpu.VMEM)] * 8,
        out_specs=[pl.BlockSpec(memory_space=pltpu.VMEM)] * 7,
        scratch_shapes=scratch,
        compiler_params=pltpu.CompilerParams(
            collective_id=2, has_side_effects=True, vmem_limit_bytes=VMEM_LIMIT
        ),
        name="train_step",
    )(tokens, cot, allow, w_qkv, w_out, w_fc, w_proj, ext)


def lanes_of(values, piece):
    return lax.rem(lax.axis_index("dp"), 128 // piece)


def pack_lanes(norm, split):
    def put(values):
        piece = values.shape[1]
        spread = jnp.tile(values, (1, 128 // piece))
        lane = jnp.arange(128) // piece
        return jnp.where(lane == lanes_of(values, piece), spread, 0.0)

    hidden = split[2:6].T.reshape(1, -1)
    packed = jnp.concatenate([hidden, put(norm), put(split[0:2])], axis=0)
    return jnp.pad(packed, ((0, EXT - packed.shape[0]), (0, 0)))


def pick_lanes(values, piece):
    return lax.dynamic_slice_in_dim(values, lanes_of(values, piece) * piece, piece, axis=1)


def by_calls(count, t, cot, allow, w_qkv, w_out, w_fc, w_proj, vec_norm, vec_split):
    rows, hidden = w_fc.shape
    width = w_qkv.shape[2]
    piece = vec_split.shape[1]
    total = t.shape[0]
    blocks = (
        w_qkv.transpose(1, 0, 2).reshape(rows, 3 * width).astype(BF),
        w_out.T.astype(BF),
        w_fc.astype(BF),
        w_proj.T.astype(BF),
        pack_ext(vec_norm, vec_split).astype(BF),
    )
    got = gather(blocks, count)
    m_qkv, m_out, m_fc, m_proj = (got[i].reshape(D, got[i].shape[2]) for i in range(4))
    vectors = got[4].astype(F32)
    bias = vectors[:, 0, : 4 * piece].reshape(1, hidden)
    norm = vectors[:, 1:7, :rows].transpose(1, 0, 2).reshape(6, D)
    split = vectors[:, 7:9, :piece].transpose(1, 0, 2).reshape(2, width)
    norm = jnp.pad(norm, ((0, 2), (0, 0)))
    split = jnp.pad(split, ((0, 6), (0, 0)))

    def swap(values):
        return lax.ppermute(values, "mp", [(0, 1), (1, 0)])

    a1, qkv, o, part = call(
        attend_body,
        "attend",
        [((total, D), BF), ((total, 3 * width), BF), ((total, width), BF), ((total, D), BF)],
        *(t, allow, norm, split, m_qkv, m_out),
    )
    r, a2, gl, dz, part2 = call(
        feed_body,
        "feed",
        [
            ((total, D), F32),
            ((total, D), BF),
            ((total, hidden), BF),
            ((total, hidden), BF),
            ((total, 2 * D), BF),
        ],
        *(t, part, swap(part), cot, norm, bias, m_fc, m_proj),
    )
    out, dr, dao, dqkv, part3, sums2 = call(
        back_body,
        "back",
        [
            ((total, D), BF),
            ((total, D), F32),
            ((total, D), BF),
            ((total, 3 * width), BF),
            ((total, D), BF),
            ((8, D), F32),
        ],
        *(part2, swap(part2), r, cot, allow, norm, qkv, m_out, m_qkv),
    )
    in_grad, sums1 = call(
        last_body,
        "last",
        [((total, D), BF), ((8, D), F32)],
        *(part3, swap(part3), t, dr, norm),
    )
    norm_sums = jnp.concatenate([sums1[0:2], sums2[0:4]], axis=0)
    stack_sums = jnp.sum(dqkv.astype(F32), axis=0)
    hidden_sums = jnp.sum(dz.astype(F32), axis=0)

    def wide(values):
        return jnp.pad(values, ((0, 0), (0, 0), (0, 128 - values.shape[2])))

    split_sums = jnp.stack([stack_sums[:width], stack_sums[2 * width :]])
    ext = jnp.concatenate(
        [
            wide(hidden_sums.reshape(count, 1, 4 * piece)),
            wide(norm_sums.reshape(6, count, rows).transpose(1, 0, 2)),
            wide(split_sums.reshape(2, count, piece).transpose(1, 0, 2)),
        ],
        axis=1,
    )
    ext = jnp.pad(ext, ((0, 0), (0, EXT - ext.shape[1]), (0, 0)))
    lhs = [v.T.reshape(count, rows, total) for v in (a1, dao, a2, cot)]
    g_qkv, g_out, g_fc, g_proj, g_ext = reduce_scatter(lhs, (dqkv, o, dz, gl), ext)
    reduced = (
        g_qkv.reshape(rows, 3, width).transpose(1, 0, 2),
        g_out.T,
        g_fc,
        g_proj.T,
        g_ext[1:7, :rows],
        jnp.concatenate([g_ext[7:9, :piece], g_ext[0, : 4 * piece].reshape(piece, 4).T]),
    )
    return out, in_grad, reduced


def by_one(count, t, cot, allow, w_qkv, w_out, w_fc, w_proj, vec_norm, vec_split):
    rows = w_fc.shape[0]
    width = w_qkv.shape[2]
    piece = vec_split.shape[1]
    ext = pack_lanes(vec_norm, vec_split)
    out, in_grad, g_qkv, g_out, g_fc, g_proj, g_ext = mega(
        count, t, cot, allow, w_qkv, w_out, w_fc, w_proj, ext
    )
    reduced = (
        g_qkv.reshape(rows, 3, width).transpose(1, 0, 2),
        g_out.T,
        g_fc,
        g_proj.T,
        pick_lanes(g_ext[1:7], rows),
        jnp.concatenate([pick_lanes(g_ext[7:9], piece), g_ext[0].reshape(piece, 4).T]),
    )
    return out, in_grad, reduced


def local(count, *args):
    (tokens, cotangent, segments, w_qkv, w_out, w_fc, w_proj, vec_norm, vec_split) = args[:9]
    firsts, seconds = args[9:15], args[15:21]
    masters = (w_qkv, w_out, w_fc, w_proj, vec_norm, vec_split)
    rows = w_fc.shape[0]
    piece = vec_split.shape[1]
    batches, length = tokens.shape[:2]
    total = batches * length
    t = tokens.reshape(total, D)
    cot = cotangent.reshape(total, D)
    seg = segments.reshape(total)
    place = jnp.arange(total)
    block = place // length
    allow = (
        (seg[:, None] == seg[None, :])
        & (block[:, None] == block[None, :])
        & (place[None, :] <= place[:, None])
    ).astype(F32)

    form = by_one if rows == 64 and 4 * piece == 128 else by_calls
    out, in_grad, reduced = form(
        count, t, cot, allow, w_qkv, w_out, w_fc, w_proj, vec_norm, vec_split
    )
    rates = rate_list()
    decays = (0.1, 0.1, 0.1, 0.1, 0.0, 0.0)
    updated = [
        adamw(masters[i], reduced[i], firsts[i], seconds[i], rates[i], decays[i])
        for i in range(6)
    ]
    return (
        out.reshape(tokens.shape),
        in_grad.reshape(tokens.shape),
        *(u[0] for u in updated),
        *(u[1] for u in updated),
        *(u[2] for u in updated),
    )


def solution(mesh):
    shards = (
        P(None, "dp", "mp"),
        P("mp", "dp"),
        P("dp", "mp"),
        P("mp", "dp"),
        P(None, "dp"),
        P(None, ("mp", "dp")),
    )
    rows = P(None, "dp", None)
    return jax.shard_map(
        functools.partial(local, mesh.shape["dp"]),
        mesh=mesh,
        in_specs=(rows, rows, P(None, "dp")) + shards * 3,
        out_specs=(rows, rows) + shards * 3,
        check_vma=False,
    )
```

```python
import functools
import math

import jax
import jax.numpy as jnp
from jax import lax
from jax.experimental import pallas as pl
from jax.experimental.pallas import tpu as pltpu
from jax.sharding import PartitionSpec as P

D = 1024
HD = 64
FF = 4096
TOK_MB = 64
STEP = 10
BF = jnp.bfloat16
F32 = jnp.float32
EXT = 16
VMEM_LIMIT = 60 * 1024 * 1024

NN = (((1,), (0,)), ((), ()))
NT = (((1,), (1,)), ((), ()))
TN = (((0,), (0,)), ((), ()))


def dot(a, b, dims=NN):
    return lax.dot_general(a, b, dims, preferred_element_type=F32)


def rate_list():
    narrow = D // min(32, max(2, TOK_MB // 4))
    return (
        2.0 / math.sqrt(D),
        2.0 / math.sqrt(narrow),
        2.0 / math.sqrt(D),
        2.0 / math.sqrt(FF),
        0.8,
        0.4,
    )


def adamw(weight, gradient, first_moment, second, step_rate, weight_decay):
    first_new = 0.9 * first_moment + 0.1 * gradient
    second_new = 0.95 * second + 0.05 * gradient * gradient
    scaled_first = first_new / (1.0 - 0.9**STEP)
    scaled_second = second_new / (1.0 - 0.95**STEP)
    weight_new = weight - step_rate * (
        scaled_first / (jnp.sqrt(scaled_second) + 1e-08) + weight_decay * weight
    )
    return (weight_new, first_new, second_new)


def make_parts(widths):
    qkv, out, fc, proj, ext = widths
    half_fc, half_proj = fc // 2, proj // 2
    return (
        (0, 0, qkv, 0),
        (2, half_fc, half_fc, 1),
        (1, 0, out, 0),
        (3, 0, half_proj, 1),
        (2, 0, half_fc, 0),
        (3, half_proj, half_proj, 1),
        (4, 0, ext, 1),
    )


def chip_at(position, chips):
    half = chips // 2
    high = lax.div(position, half)
    return (1 - high) * 2 * position + high * (2 * (chips - 1 - position) + 1)


def position_of(chip, chips):
    odd = lax.rem(chip, 2)
    row = lax.div(chip, 2)
    return (1 - odd) * row + odd * (chips - 1 - row)


def ring_place(chips):
    me = lax.axis_index("dp")
    core = lax.rem(me, 2)
    place = position_of(lax.div(me, 2), chips)

    def device(position):
        return chip_at(lax.rem(position + 2 * chips, chips), chips) * 2 + core

    return me, me + 1 - 2 * core, place, device


def greet(others):
    barrier = pltpu.get_barrier_semaphore()
    for other in others:
        pl.semaphore_signal(
            barrier, inc=1, device_id=other, device_id_type=pl.DeviceIdType.MESH
        )
    pl.semaphore_wait(barrier, len(others))


def remote(src, dst, send, recv, target):
    return pltpu.make_async_remote_copy(
        src_ref=src,
        dst_ref=dst,
        send_sem=send,
        recv_sem=recv,
        device_id={"dp": target},
        device_id_type=pl.DeviceIdType.MESH,
    )


def gather_kernel(chips, parts, *refs):
    ins, outs = refs[:5], refs[5:10]
    ring_send, ring_recv, side_send, side_recv = refs[10:]
    me, sibling, place, device = ring_place(chips)
    neighbours = (device(place + 1), device(place - 1))
    greet([{"dp": neighbours[0]}, {"dp": neighbours[1]}, {"dp": sibling}])
    for index in range(5):
        outs[index][me] = ins[index][...]

    def ring_copy(k, step):
        index, first, wide, way = parts[k]
        owner = device(place - step if way == 0 else place + step)
        block = outs[index].at[owner, :, pl.ds(first, wide)]
        return remote(
            block, block, ring_send.at[k, step], ring_recv.at[k, step], neighbours[way]
        )

    def side_copy(k, step):
        index, first, wide, way = parts[k]
        owner = device(place - step if way == 0 else place + step)
        block = outs[index].at[owner, :, pl.ds(first, wide)]
        return remote(block, block, side_send.at[k, step], side_recv.at[k, step], sibling)

    for k in range(len(parts)):
        ring_copy(k, 0).start()
    for k in range(len(parts)):
        side_copy(k, 0).start()

    @pl.loop(1, chips - 1)
    def _(step):
        for k in range(len(parts)):
            ring_copy(k, step - 1).wait_recv()
            ring_copy(k, step).start()
            side_copy(k, step).start()

    for k in range(len(parts)):
        ring_copy(k, chips - 2).wait_recv()
        side_copy(k, chips - 1).start()

    @pl.loop(0, chips - 1)
    def _(step):
        for k in range(len(parts)):
            ring_copy(k, step).wait_send()

    @pl.loop(0, chips)
    def _(step):
        for k in range(len(parts)):
            side_copy(k, step).wait()


def gather(blocks, count):
    chips = count // 2
    parts = make_parts([block.shape[1] for block in blocks])
    sems = [
        pltpu.SemaphoreType.DMA((len(parts), chips - 1)),
        pltpu.SemaphoreType.DMA((len(parts), chips - 1)),
        pltpu.SemaphoreType.DMA((len(parts), chips)),
        pltpu.SemaphoreType.DMA((len(parts), chips)),
    ]
    return pl.pallas_call(
        functools.partial(gather_kernel, chips, parts),
        out_shape=[jax.ShapeDtypeStruct((count,) + b.shape, b.dtype) for b in blocks],
        in_specs=[pl.BlockSpec(memory_space=pltpu.VMEM)] * 5,
        out_specs=[pl.BlockSpec(memory_space=pltpu.VMEM)] * 5,
        scratch_shapes=sems,
        compiler_params=pltpu.CompilerParams(
            collective_id=0, has_side_effects=True, vmem_limit_bytes=VMEM_LIMIT
        ),
        name="gather_weights",
    )(*blocks)


def reduce_kernel(chips, parts, *refs):
    lhs, rhs, ext = refs[:4], refs[4:8], refs[8]
    outs = refs[9:14]
    bufs = refs[14:19]
    terms = refs[19:24]
    left, right = refs[24:28], refs[28:32]
    ext_other = refs[32]
    ring_send, ring_recv, side_send, side_recv, local_sem = refs[33:]
    tokens = rhs[0].shape[0]
    me, sibling, place, device = ring_place(chips)
    neighbours = (device(place + 1), device(place - 1))
    greet([{"dp": neighbours[0]}, {"dp": neighbours[1]}, {"dp": sibling}])
    sides = []
    locals_ = []
    for m in range(4):
        sides.append(
            remote(
                lhs[m],
                left[m].at[:, :, pl.ds(tokens, tokens)],
                side_send.at[2 * m],
                side_recv.at[2 * m],
                sibling,
            )
        )
        sides.append(
            remote(
                rhs[m],
                right[m].at[pl.ds(tokens, tokens)],
                side_send.at[2 * m + 1],
                side_recv.at[2 * m + 1],
                sibling,
            )
        )
        locals_.append(
            pltpu.make_async_copy(
                lhs[m], left[m].at[:, :, pl.ds(0, tokens)], local_sem.at[2 * m]
            )
        )
        locals_.append(
            pltpu.make_async_copy(
                rhs[m], right[m].at[pl.ds(0, tokens)], local_sem.at[2 * m + 1]
            )
        )
    sides.append(remote(ext, ext_other, side_send.at[8], side_recv.at[8], sibling))
    for copy in sides:
        copy.start()
    for copy in locals_:
        copy.start()
    for copy in sides:
        copy.wait()
    for copy in locals_:
        copy.wait()

    def owner_of(k, step):
        way = parts[k][3]
        return device(place - 1 - step if way == 0 else place + 1 + step)

    def term(k, step):
        index, first, wide, _ = parts[k]
        owner = owner_of(k, step)
        if index == 4:
            return ext[owner] + ext_other[owner]
        return dot(left[index][owner], right[index][:, pl.ds(first, wide)])

    def ring_copy(k, step):
        index, first, wide, way = parts[k]
        columns = pl.ds(first, wide)
        return remote(
            bufs[index].at[step, :, columns],
            bufs[index].at[step + 1, :, columns],
            ring_send.at[k, step],
            ring_recv.at[k, step],
            neighbours[way],
        )

    for k in range(len(parts)):
        index, first, wide, _ = parts[k]
        bufs[index][0, :, pl.ds(first, wide)] = term(k, 0).astype(BF)
        ring_copy(k, 0).start()

    def fill(step):
        for k in range(len(parts)):
            index, first, wide, _ = parts[k]
            terms[index][:, pl.ds(first, wide)] = term(k, step)

    @pl.loop(1, chips - 1)
    def _(step):
        fill(step)
        for k in range(len(parts)):
            index, first, wide, _ = parts[k]
            columns = pl.ds(first, wide)
            ring_copy(k, step - 1).wait_recv()
            bufs[index][step, :, columns] = (
                bufs[index][step, :, columns].astype(F32) + terms[index][:, columns]
            ).astype(BF)
            ring_copy(k, step).start()

    fill(chips - 1)
    for k in range(len(parts)):
        index, first, wide, _ = parts[k]
        columns = pl.ds(first, wide)
        ring_copy(k, chips - 2).wait_recv()
        outs[index][:, columns] = (
            bufs[index][chips - 1, :, columns].astype(F32) + terms[index][:, columns]
        )

    @pl.loop(0, chips - 1)
    def _(step):
        for k in range(len(parts)):
            ring_copy(k, step).wait_send()


def reduce_scatter(lhs, rhs, ext):
    count, rows, tokens = lhs[0].shape
    chips = count // 2
    widths = [r.shape[1] for r in rhs] + [ext.shape[2]]
    heights = [rows] * 4 + [ext.shape[1]]
    parts = make_parts(widths)
    scratch = [pltpu.VMEM((chips, h, w), BF) for h, w in zip(heights, widths)]
    scratch += [pltpu.VMEM((h, w), F32) for h, w in zip(heights, widths)]
    scratch += [pltpu.VMEM((count, rows, 2 * tokens), BF) for _ in range(4)]
    scratch += [pltpu.VMEM((2 * tokens, w), BF) for w in widths[:4]]
    scratch += [pltpu.VMEM(ext.shape, F32)]
    scratch += [
        pltpu.SemaphoreType.DMA((len(parts), chips - 1)),
        pltpu.SemaphoreType.DMA((len(parts), chips - 1)),
        pltpu.SemaphoreType.DMA((9,)),
        pltpu.SemaphoreType.DMA((9,)),
        pltpu.SemaphoreType.DMA((8,)),
    ]
    return pl.pallas_call(
        functools.partial(reduce_kernel, chips, parts),
        out_shape=[jax.ShapeDtypeStruct((h, w), F32) for h, w in zip(heights, widths)],
        in_specs=[pl.BlockSpec(memory_space=pltpu.VMEM)] * 9,
        out_specs=[pl.BlockSpec(memory_space=pltpu.VMEM)] * 5,
        scratch_shapes=scratch,
        compiler_params=pltpu.CompilerParams(
            collective_id=1, has_side_effects=True, vmem_limit_bytes=VMEM_LIMIT
        ),
        name="reduce_gradients",
    )(*lhs, *rhs, ext)


def normalize(values):
    center = values - jnp.mean(values, axis=-1, keepdims=True)
    spread = jnp.mean(center * center, axis=-1, keepdims=True)
    scale = lax.rsqrt(spread + 1e-05)
    return center * scale, scale


def normalize_back(grad, gain, unit, scale):
    inner = grad * gain
    return scale * (
        inner
        - jnp.mean(inner, axis=-1, keepdims=True)
        - unit * jnp.mean(inner * unit, axis=-1, keepdims=True)
    )


def head_mask(shape, which):
    lane = lax.broadcasted_iota(jnp.int32, shape, 1)
    return lax.div(lane, HD) == which


def head_probs(query, key, which, allowed):
    only = jnp.where(head_mask(query.shape, which), query, jnp.zeros_like(query))
    scores = jnp.where(allowed, dot(only, key, NT) * 0.125, -1000000000.0)
    exponent = jnp.exp(scores - jnp.max(scores, axis=-1, keepdims=True))
    return exponent / jnp.sum(exponent, axis=-1, keepdims=True)


def attend_body(tokens, allow, norm, split, w_qkv, w_out, a1, qkv, o, part):
    width = o.shape[1]
    unit, _ = normalize(tokens[...].astype(F32))
    a1[...] = (unit * norm[0:1] + norm[1:2]).astype(BF)
    for t in range(3):
        columns = pl.ds(t * width, width)
        rows = dot(a1[...], w_qkv[:, columns])
        if t != 1:
            rows = rows + split[pl.ds(t // 2, 1)]
        qkv[:, columns] = rows.astype(BF)
    allowed = allow[...] > 0.5
    for pair in range(width // (2 * HD)):
        first = pair * 2 * HD
        query, key, value = (
            qkv[:, pl.ds(t * width + first, 2 * HD)] for t in range(3)
        )
        total = jnp.zeros(query.shape, F32)
        for which in range(2):
            probs = head_probs(query, key, which, allowed).astype(BF)
            only = jnp.where(head_mask(value.shape, which), value, jnp.zeros_like(value))
            total = total + dot(probs, only)
        o[:, pl.ds(first, 2 * HD)] = total.astype(BF)
    part[...] = dot(o[...], w_out[...], NT).astype(BF)


def feed_body(
    tokens, mine, other, cot, norm, bias, w_fc, w_proj, r, a2, gl, dz, part
):
    rows = tokens[...].astype(F32) + (mine[...].astype(F32) + other[...].astype(F32))
    rows = rows + norm[4:5]
    r[...] = rows
    unit, _ = normalize(rows)
    a2[...] = (unit * norm[2:3] + norm[3:4]).astype(BF)
    width = gl.shape[1]
    step = 512
    root = math.sqrt(2.0 / math.pi)
    for first in range(0, width, step):
        columns = pl.ds(first, step)
        z = dot(a2[...], w_fc[:, columns]) + bias[:, columns]
        bent = jnp.tanh(root * (z + 0.044715 * z * z * z))
        gl[:, columns] = (0.5 * z * (1.0 + bent)).astype(BF)
        slope = 0.5 * (1.0 + bent) + 0.5 * z * (1.0 - bent * bent) * root * (
            1.0 + 3.0 * 0.044715 * z * z
        )
        dz[:, columns] = (slope * dot(cot[...], w_proj[:, columns])).astype(BF)
    part[:, pl.ds(0, D)] = dot(gl[...], w_proj[...], NT).astype(BF)
    part[:, pl.ds(D, D)] = dot(dz[...], w_fc[...], NT).astype(BF)


def back_body(
    mine, other, r, cot, allow, norm, qkv, w_out, w_qkv, out, dr, dao, dqkv, part, sums
):
    total = mine[...].astype(F32) + other[...].astype(F32)
    rows = r[...]
    out[...] = (rows + total[:, :D] + norm[5:6]).astype(BF)
    da2 = total[:, D:]
    unit, scale = normalize(rows)
    top = cot[...].astype(F32)
    grad = top + normalize_back(da2, norm[2:3], unit, scale)
    dr[...] = grad
    dao[...] = grad.astype(BF)
    sums[0:1] = jnp.sum(da2 * unit, axis=0, keepdims=True)
    sums[1:2] = jnp.sum(da2, axis=0, keepdims=True)
    sums[2:3] = jnp.sum(grad, axis=0, keepdims=True)
    sums[3:4] = jnp.sum(top, axis=0, keepdims=True)
    sums[4:8] = jnp.zeros((4, D), F32)
    width = w_out.shape[1]
    heads = dot(dao[...], w_out[...]).astype(BF)
    allowed = allow[...] > 0.5
    for pair in range(width // (2 * HD)):
        first = pair * 2 * HD
        query, key, value = (
            qkv[:, pl.ds(t * width + first, 2 * HD)] for t in range(3)
        )
        do = heads[:, first : first + 2 * HD]
        zero = jnp.zeros_like(query)
        dq = jnp.zeros(query.shape, F32)
        dk = jnp.zeros(query.shape, F32)
        dv = jnp.zeros(query.shape, F32)
        for which in range(2):
            mask = head_mask(query.shape, which)
            probs = head_probs(query, key, which, allowed)
            only = jnp.where(mask, do, zero)
            dp = dot(only, value, NT)
            ds = probs * (dp - jnp.sum(probs * dp, axis=-1, keepdims=True))
            ds = ds.astype(BF)
            dq = dq + dot(ds, jnp.where(mask, key, zero))
            dk = dk + dot(ds, jnp.where(mask, query, zero), TN)
            dv = dv + dot(probs.astype(BF), only, TN)
        dqkv[:, pl.ds(first, 2 * HD)] = (dq * 0.125).astype(BF)
        dqkv[:, pl.ds(width + first, 2 * HD)] = (dk * 0.125).astype(BF)
        dqkv[:, pl.ds(2 * width + first, 2 * HD)] = dv.astype(BF)
    part[...] = dot(dqkv[...], w_qkv[...], NT).astype(BF)


def last_body(mine, other, tokens, dr, norm, grad, sums):
    da1 = mine[...].astype(F32) + other[...].astype(F32)
    unit, scale = normalize(tokens[...].astype(F32))
    grad[...] = (dr[...] + normalize_back(da1, norm[0:1], unit, scale)).astype(BF)
    sums[0:1] = jnp.sum(da1 * unit, axis=0, keepdims=True)
    sums[1:2] = jnp.sum(da1, axis=0, keepdims=True)
    sums[2:8] = jnp.zeros((6, D), F32)


def call(body, name, shapes, *args):
    return pl.pallas_call(
        body,
        out_shape=[jax.ShapeDtypeStruct(s, d) for s, d in shapes],
        in_specs=[pl.BlockSpec(memory_space=pltpu.VMEM)] * len(args),
        out_specs=[pl.BlockSpec(memory_space=pltpu.VMEM)] * len(shapes),
        compiler_params=pltpu.CompilerParams(vmem_limit_bytes=VMEM_LIMIT),
        name=name,
    )(*args)


def pack_ext(norm, split):
    rows, columns = norm.shape[1], split.shape[1]

    def wide(values):
        return jnp.pad(values, ((0, 0), (0, 128 - values.shape[1])))

    hidden = split[2:6].T.reshape(1, 4 * columns)
    packed = jnp.concatenate([wide(hidden), wide(norm), wide(split[0:2])], axis=0)
    return jnp.pad(packed, ((0, EXT - packed.shape[0]), (0, 0)))


def mega_kernel(chips, *refs):
    (tokens, cot, allow, i_qkv, i_out, i_fc, i_proj, i_ext) = refs[:8]
    out, grad = refs[8:10]
    outs = refs[10:15]
    full = refs[15:20]
    bufs = refs[20:25]
    terms = refs[25:30]
    left, right = refs[30:34], refs[34:38]
    (norm, split, bias, qkv, r, a2, slope, dr, ext, ext_other) = refs[38:48]
    mine, other = refs[48:52], refs[52:56]
    (g_send, g_recv, gs_send, gs_recv, r_send, r_recv, s_send, s_recv, m_send, m_recv) = refs[56:]

    count = 2 * chips
    rows = i_fc.shape[0]
    total = tokens.shape[0]
    width = i_out.shape[1]
    hidden = i_fc.shape[1]
    me, sibling, place, device = ring_place(chips)
    peer = 1 - lax.axis_index("mp")
    neighbours = (device(place + 1), device(place - 1))
    greet(
        [{"dp": neighbours[0]}, {"dp": neighbours[1]}, {"dp": sibling}, {"mp": peer}]
    )

    h_qkv, h_out, q_ff = 3 * width // 2, width // 2, hidden // 4
    groups = (
        [(4, 0, 128, 0), (0, 0, h_qkv, 0), (0, h_qkv, h_qkv, 1)]
        + [(1, 0, h_out, 0), (1, h_out, h_out, 1)],
        [(2, j * q_ff, q_ff, j % 2) for j in range(4)],
        [(3, j * q_ff, q_ff, j % 2) for j in range(4)],
    )
    parts, members = [], []
    for group in groups:
        members.append(list(range(len(parts), len(parts) + len(group))))
        parts += group

    def rows_of(index, owner):
        high = EXT if index == 4 else rows
        return pl.ds(pl.multiple_of(owner * high, high), high)

    def block(k, step):
        index, first, wide, way = parts[k]
        owner = device(place - step if way == 0 else place + step)
        return full[index].at[rows_of(index, owner), pl.ds(first, wide)]

    def ring_copy(k, step):
        ref = block(k, step)
        return remote(ref, ref, g_send.at[k, step], g_recv.at[k, step], neighbours[parts[k][3]])

    def side_copy(k, step):
        ref = block(k, step)
        return remote(ref, ref, gs_send.at[k, step], gs_recv.at[k, step], sibling)

    def gather_step(group, step):
        for k in members[group]:
            if step > 0:
                ring_copy(k, step - 1).wait_recv()
            if step < chips - 1:
                ring_copy(k, step).start()
            side_copy(k, step).start()

    def gather_end(group):
        for k in members[group]:
            for step in range(chips):
                side_copy(k, step).wait_recv()

    def to_side(m):
        pairs = (
            (left[m].at[:, pl.ds(0, total)], left[m].at[:, pl.ds(total, total)]),
            (right[m].at[pl.ds(0, total)], right[m].at[pl.ds(total, total)]),
        )
        return [
            remote(src, dst, s_send.at[2 * m + j], s_recv.at[2 * m + j], sibling)
            for j, (src, dst) in enumerate(pairs)
        ]

    side_ext = remote(ext, ext_other, s_send.at[8], s_recv.at[8], sibling)

    def to_peer(j):
        return pltpu.make_async_remote_copy(
            src_ref=mine[j],
            dst_ref=other[j],
            send_sem=m_send.at[j],
            recv_sem=m_recv.at[j],
            device_id={"mp": peer},
            device_id_type=pl.DeviceIdType.MESH,
        )

    def flip(values):
        return values.astype(F32).T.astype(BF)

    def reduce_rows(index, k, step):
        way = parts[k][3]
        owner = device(place - 1 - step if way == 0 else place + 1 + step)
        return rows_of(index, owner)

    def term(k, step):
        index, first, wide, _ = parts[k]
        at = reduce_rows(index, k, step)
        if index == 4:
            return ext[at, :] + ext_other[at, :]
        return dot(left[index][at, :], right[index][:, pl.ds(first, wide)])

    def sum_copy(k, step):
        index, first, wide, way = parts[k]
        columns = pl.ds(first, wide)
        return remote(
            bufs[index].at[step, :, columns],
            bufs[index].at[step + 1, :, columns],
            r_send.at[k, step],
            r_recv.at[k, step],
            neighbours[way],
        )

    def reduce_step(ks, step):
        if step == 0:
            for k in ks:
                index, first, wide, _ = parts[k]
                bufs[index][0, :, pl.ds(first, wide)] = term(k, 0).astype(BF)
                sum_copy(k, 0).start()
            return
        for k in ks:
            index, first, wide, _ = parts[k]
            terms[index][:, pl.ds(first, wide)] = term(k, step)
        for k in ks:
            index, first, wide, _ = parts[k]
            columns = pl.ds(first, wide)
            sum_copy(k, step - 1).wait_recv()
            value = bufs[index][step, :, columns].astype(F32) + terms[index][:, columns]
            if step < chips - 1:
                bufs[index][step, :, columns] = value.astype(BF)
                sum_copy(k, step).start()
            else:
                outs[index][:, columns] = value

    own = rows_of(0, me)
    full[4][rows_of(4, me), :] = i_ext[...].astype(BF)
    for t in range(3):
        full[0][own, pl.ds(t * width, width)] = i_qkv[t].astype(BF)
    full[1][own, :] = i_out[...].astype(BF)
    gather_step(0, 0)
    full[2][own, :] = i_fc[...].astype(BF)
    full[3][own, :] = i_proj[...].astype(BF)
    left[3][:, pl.ds(0, total)] = flip(cot[...])
    here = pl.ds(0, total)

    def vectors():
        for j in range(count):
            bias[:, pl.ds(j * 128, 128)] = full[4][pl.ds(j * EXT, EXT), :].astype(F32)
        each = 128 // rows
        for j in range(count // each):
            norm[:, pl.ds(j * 128, 128)] = sum(
                full[4][pl.ds((j * each + i) * EXT, EXT), :].astype(F32) for i in range(each)
            )
        each = count * 128 // width
        for j in range(count // each):
            split[:, pl.ds(j * 128, 128)] = sum(
                full[4][pl.ds((j * each + i) * EXT, EXT), :].astype(F32) for i in range(each)
            )

    def first_norm():
        vectors()
        unit, _ = normalize(tokens[...].astype(F32))
        mine[0][...] = (unit * norm[1:2] + norm[2:3]).astype(BF)
        left[0][:, here] = flip(mine[0][...])

    def project(t):
        columns = pl.ds(t * width, width)
        values = dot(mine[0][...], full[0][:, columns])
        if t != 1:
            values = values + split[pl.ds(7 + t // 2, 1)]
        qkv[:, columns] = values.astype(BF)

    def heads_of(pair):
        first = pair * 2 * HD
        return [qkv[:, pl.ds(t * width + first, 2 * HD)] for t in range(3)]

    def attend(pair):
        query, key, value = heads_of(pair)
        allowed = allow[...] > 0.5
        result = jnp.zeros(query.shape, F32)
        for which in range(2):
            probs = head_probs(query, key, which, allowed).astype(BF)
            only = jnp.where(head_mask(value.shape, which), value, jnp.zeros_like(value))
            result = result + dot(probs, only)
        right[1][here, pl.ds(pair * 2 * HD, 2 * HD)] = result.astype(BF)

    def attend_out():
        mine[0][...] = dot(right[1][here, :], full[1][...], NT).astype(BF)
        to_peer(0).start()

    def second_norm():
        to_peer(0).wait()
        values = tokens[...].astype(F32) + (mine[0][...].astype(F32) + other[0][...].astype(F32))
        values = values + norm[5:6]
        r[...] = values
        unit, _ = normalize(values)
        a2[...] = (unit * norm[3:4] + norm[4:5]).astype(BF)
        left[2][:, here] = flip(a2[...])

    root = math.sqrt(2.0 / math.pi)

    def gelu(j):
        columns = pl.ds(j * q_ff, q_ff)
        z = dot(a2[...], full[2][:, columns]) + bias[0:1, columns]
        bent = jnp.tanh(root * (z + 0.044715 * z * z * z))
        right[3][here, columns] = (0.5 * z * (1.0 + bent)).astype(BF)
        slope[:, columns] = 0.5 * (1.0 + bent) + 0.5 * z * (1.0 - bent * bent) * root * (
            1.0 + 3.0 * 0.044715 * z * z
        )

    def start_all(copies):
        for copy in copies:
            copy.start()

    def wait_all(copies):
        for copy in copies:
            copy.wait()

    pairs = width // (2 * HD)
    lag = 3
    units = [
        [lambda: gather_end(0), first_norm, lambda: project(0)],
        [lambda: project(1), lambda: project(2)]
        + [lambda j=j: attend(j) for j in range(pairs // 2)],
        [lambda j=j: attend(j) for j in range(pairs // 2, pairs)] + [attend_out],
        [lambda: gather_end(1)],
        [second_norm, lambda: gelu(0)],
        [lambda: gelu(1), lambda: gelu(2)],
        [lambda: gelu(3), lambda: start_all(to_side(3))],
    ]
    for tick in range(chips + max(2 * lag, len(units))):
        for group in range(3):
            step = tick - lag * group
            if 0 <= step < chips and (group, step) != (0, 0):
                gather_step(group, step)
        if 0 <= tick - chips < len(units):
            for unit in units[tick - chips]:
                unit()
    gather_end(2)

    def gate_back(j):
        columns = pl.ds(j * q_ff, q_ff)
        right[2][here, columns] = (
            slope[:, columns] * dot(cot[...], full[3][:, columns])
        ).astype(BF)

    def feed_back():
        mine[1][...] = dot(right[2][here, :], full[2][...], NT).astype(BF)
        to_peer(1).start()

    def feed_out():
        mine[3][...] = dot(right[3][here, :], full[3][...], NT).astype(BF)
        to_peer(3).start()

    def finish_out():
        to_peer(3).wait()
        both = mine[3][...].astype(F32) + other[3][...].astype(F32)
        out[...] = (r[...] + both + norm[6:7]).astype(BF)

    def second_back():
        to_peer(1).wait()
        da2 = mine[1][...].astype(F32) + other[1][...].astype(F32)
        unit, scale = normalize(r[...])
        top = cot[...].astype(F32)
        value = top + normalize_back(da2, norm[3:4], unit, scale)
        dr[...] = value
        a2[...] = value.astype(BF)
        left[1][:, here] = flip(a2[...])
        sums = [da2 * unit, da2, value, top]
        for j in range(4):
            line = jnp.sum(sums[j], axis=0, keepdims=True)
            for d in range(count):
                ext[pl.ds(d * EXT + 3 + j, 1), :] = line[:, d * rows // 128 * 128 :][:, :128]

    def heads_back():
        mine[2][:, pl.ds(0, width)] = dot(a2[...], full[1][...]).astype(BF)

    def attend_back(pair):
        query, key, value = heads_of(pair)
        first = pair * 2 * HD
        do = mine[2][:, pl.ds(first, 2 * HD)]
        allowed = allow[...] > 0.5
        zero = jnp.zeros_like(query)
        dq = jnp.zeros(query.shape, F32)
        dk = jnp.zeros(query.shape, F32)
        dv = jnp.zeros(query.shape, F32)
        for which in range(2):
            mask = head_mask(query.shape, which)
            probs = head_probs(query, key, which, allowed)
            only = jnp.where(mask, do, zero)
            dp = dot(only, value, NT)
            ds = probs * (dp - jnp.sum(probs * dp, axis=-1, keepdims=True))
            ds = ds.astype(BF)
            dq = dq + dot(ds, jnp.where(mask, key, zero))
            dk = dk + dot(ds, jnp.where(mask, query, zero), TN)
            dv = dv + dot(probs.astype(BF), only, TN)
        right[0][here, pl.ds(first, 2 * HD)] = (dq * 0.125).astype(BF)
        right[0][here, pl.ds(width + first, 2 * HD)] = (dk * 0.125).astype(BF)
        right[0][here, pl.ds(2 * width + first, 2 * HD)] = dv.astype(BF)

    def attend_in():
        mine[2][...] = dot(right[0][here, :], full[0][...], NT).astype(BF)
        to_peer(2).start()

    def first_back():
        to_peer(2).wait()
        da1 = mine[2][...].astype(F32) + other[2][...].astype(F32)
        unit, scale = normalize(tokens[...].astype(F32))
        grad[...] = (dr[...] + normalize_back(da1, norm[1:2], unit, scale)).astype(BF)
        lines = [jnp.sum(da1 * unit, axis=0, keepdims=True), jnp.sum(da1, axis=0, keepdims=True)]
        heads = jnp.sum(right[0][here, :].astype(F32), axis=0, keepdims=True)
        gates = jnp.sum(right[2][here, :].astype(F32), axis=0, keepdims=True)
        each = count * 128 // width
        for d in range(count):
            ext[pl.ds(d * EXT, 1), :] = gates[:, d * 128 : (d + 1) * 128]
            for j in range(2):
                ext[pl.ds(d * EXT + 1 + j, 1), :] = lines[j][:, d * rows // 128 * 128 :][:, :128]
                at = 2 * j * width + d // each * 128
                ext[pl.ds(d * EXT + 7 + j, 1), :] = heads[:, at : at + 128]
        side_ext.start()

    ext[...] = jnp.zeros(ext.shape, F32)
    waves = (
        (members[2], 0, lambda: wait_all(to_side(3))),
        (members[1], 2, lambda: wait_all(to_side(2))),
        (members[0][3:], 5, lambda: wait_all(to_side(1))),
        (members[0][1:3], 7, lambda: wait_all(to_side(0))),
        (members[0][:1], 8, side_ext.wait),
    )
    units = [
        [lambda j=j: gate_back(j) for j in range(4)] + [lambda: start_all(to_side(2))],
        [feed_back],
        [feed_out],
        [second_back, lambda: start_all(to_side(1))],
        [heads_back] + [lambda j=j: attend_back(j) for j in range(pairs // 2)],
        [lambda j=j: attend_back(j) for j in range(pairs // 2, pairs)]
        + [lambda: start_all(to_side(0)), attend_in],
        [finish_out],
        [first_back],
    ]
    for tick in range(8 + chips):
        for ks, begin, ready in waves:
            step = tick - begin
            if step == 0:
                ready()
            if 0 <= step < chips:
                reduce_step(ks, step)
        if tick < len(units):
            for unit in units[tick]:
                unit()

    for k in range(len(parts)):
        for step in range(chips - 1):
            ring_copy(k, step).wait_send()
            sum_copy(k, step).wait_send()
        for step in range(chips):
            side_copy(k, step).wait_send()


def mega(count, tokens, cot, allow, w_qkv, w_out, w_fc, w_proj, ext):
    chips = count // 2
    total = tokens.shape[0]
    rows, hidden = w_fc.shape
    width = w_out.shape[1]
    widths = (3 * width, width, hidden, hidden, 128)
    heights = (rows, rows, rows, rows, EXT)
    scratch = [pltpu.VMEM((count * h, w), BF) for h, w in zip(heights, widths)]
    scratch += [pltpu.VMEM((chips, h, w), BF) for h, w in zip(heights, widths)]
    scratch += [pltpu.VMEM((h, w), F32) for h, w in zip(heights, widths)]
    scratch += [pltpu.VMEM((D, 2 * total), BF) for _ in range(4)]
    scratch += [pltpu.VMEM((2 * total, w), BF) for w in widths[:4]]
    scratch += [
        pltpu.VMEM((EXT, D), F32),
        pltpu.VMEM((EXT, width), F32),
        pltpu.VMEM((EXT, hidden), F32),
        pltpu.VMEM((total, 3 * width), BF),
        pltpu.VMEM((total, D), F32),
        pltpu.VMEM((total, D), BF),
        pltpu.VMEM((total, hidden), F32),
        pltpu.VMEM((total, D), F32),
        pltpu.VMEM((count * EXT, 128), F32),
        pltpu.VMEM((count * EXT, 128), F32),
    ]
    scratch += [pltpu.VMEM((total, w), BF) for w in (D, D, D, D)] * 2
    n_parts = 13
    sem = pltpu.SemaphoreType.DMA
    scratch += [sem((n_parts, chips - 1))] * 2 + [sem((n_parts, chips))] * 2
    scratch += [sem((n_parts, chips - 1))] * 2 + [sem((9,))] * 2 + [sem((4,))] * 2
    shapes = [((total, D), BF)] * 2 + [((h, w), F32) for h, w in zip(heights, widths)]
    return pl.pallas_call(
        functools.partial(mega_kernel, chips),
        out_shape=[jax.ShapeDtypeStruct(s, d) for s, d in shapes],
        in_specs=[pl.BlockSpec(memory_space=pltpu.VMEM)] * 8,
        out_specs=[pl.BlockSpec(memory_space=pltpu.VMEM)] * 7,
        scratch_shapes=scratch,
        compiler_params=pltpu.CompilerParams(
            collective_id=2, has_side_effects=True, vmem_limit_bytes=VMEM_LIMIT
        ),
        name="train_step",
    )(tokens, cot, allow, w_qkv, w_out, w_fc, w_proj, ext)


def lanes_of(values, piece):
    return lax.rem(lax.axis_index("dp"), 128 // piece)


def pack_lanes(norm, split):
    def put(values):
        piece = values.shape[1]
        spread = jnp.tile(values, (1, 128 // piece))
        lane = jnp.arange(128) // piece
        return jnp.where(lane == lanes_of(values, piece), spread, 0.0)

    hidden = split[2:6].T.reshape(1, -1)
    packed = jnp.concatenate([hidden, put(norm), put(split[0:2])], axis=0)
    return jnp.pad(packed, ((0, EXT - packed.shape[0]), (0, 0)))


def pick_lanes(values, piece):
    return lax.dynamic_slice_in_dim(values, lanes_of(values, piece) * piece, piece, axis=1)


def by_calls(count, t, cot, allow, w_qkv, w_out, w_fc, w_proj, vec_norm, vec_split):
    rows, hidden = w_fc.shape
    width = w_qkv.shape[2]
    piece = vec_split.shape[1]
    total = t.shape[0]
    blocks = (
        w_qkv.transpose(1, 0, 2).reshape(rows, 3 * width).astype(BF),
        w_out.T.astype(BF),
        w_fc.astype(BF),
        w_proj.T.astype(BF),
        pack_ext(vec_norm, vec_split).astype(BF),
    )
    got = gather(blocks, count)
    m_qkv, m_out, m_fc, m_proj = (got[i].reshape(D, got[i].shape[2]) for i in range(4))
    vectors = got[4].astype(F32)
    bias = vectors[:, 0, : 4 * piece].reshape(1, hidden)
    norm = vectors[:, 1:7, :rows].transpose(1, 0, 2).reshape(6, D)
    split = vectors[:, 7:9, :piece].transpose(1, 0, 2).reshape(2, width)
    norm = jnp.pad(norm, ((0, 2), (0, 0)))
    split = jnp.pad(split, ((0, 6), (0, 0)))

    def swap(values):
        return lax.ppermute(values, "mp", [(0, 1), (1, 0)])

    a1, qkv, o, part = call(
        attend_body,
        "attend",
        [((total, D), BF), ((total, 3 * width), BF), ((total, width), BF), ((total, D), BF)],
        *(t, allow, norm, split, m_qkv, m_out),
    )
    r, a2, gl, dz, part2 = call(
        feed_body,
        "feed",
        [
            ((total, D), F32),
            ((total, D), BF),
            ((total, hidden), BF),
            ((total, hidden), BF),
            ((total, 2 * D), BF),
        ],
        *(t, part, swap(part), cot, norm, bias, m_fc, m_proj),
    )
    out, dr, dao, dqkv, part3, sums2 = call(
        back_body,
        "back",
        [
            ((total, D), BF),
            ((total, D), F32),
            ((total, D), BF),
            ((total, 3 * width), BF),
            ((total, D), BF),
            ((8, D), F32),
        ],
        *(part2, swap(part2), r, cot, allow, norm, qkv, m_out, m_qkv),
    )
    in_grad, sums1 = call(
        last_body,
        "last",
        [((total, D), BF), ((8, D), F32)],
        *(part3, swap(part3), t, dr, norm),
    )
    norm_sums = jnp.concatenate([sums1[0:2], sums2[0:4]], axis=0)
    stack_sums = jnp.sum(dqkv.astype(F32), axis=0)
    hidden_sums = jnp.sum(dz.astype(F32), axis=0)

    def wide(values):
        return jnp.pad(values, ((0, 0), (0, 0), (0, 128 - values.shape[2])))

    split_sums = jnp.stack([stack_sums[:width], stack_sums[2 * width :]])
    ext = jnp.concatenate(
        [
            wide(hidden_sums.reshape(count, 1, 4 * piece)),
            wide(norm_sums.reshape(6, count, rows).transpose(1, 0, 2)),
            wide(split_sums.reshape(2, count, piece).transpose(1, 0, 2)),
        ],
        axis=1,
    )
    ext = jnp.pad(ext, ((0, 0), (0, EXT - ext.shape[1]), (0, 0)))
    lhs = [v.T.reshape(count, rows, total) for v in (a1, dao, a2, cot)]
    g_qkv, g_out, g_fc, g_proj, g_ext = reduce_scatter(lhs, (dqkv, o, dz, gl), ext)
    reduced = (
        g_qkv.reshape(rows, 3, width).transpose(1, 0, 2),
        g_out.T,
        g_fc,
        g_proj.T,
        g_ext[1:7, :rows],
        jnp.concatenate([g_ext[7:9, :piece], g_ext[0, : 4 * piece].reshape(piece, 4).T]),
    )
    return out, in_grad, reduced


def by_one(count, t, cot, allow, w_qkv, w_out, w_fc, w_proj, vec_norm, vec_split):
    rows = w_fc.shape[0]
    width = w_qkv.shape[2]
    piece = vec_split.shape[1]
    ext = pack_lanes(vec_norm, vec_split)
    out, in_grad, g_qkv, g_out, g_fc, g_proj, g_ext = mega(
        count, t, cot, allow, w_qkv, w_out.T, w_fc, w_proj.T, ext
    )
    reduced = (
        g_qkv.reshape(rows, 3, width).transpose(1, 0, 2),
        g_out.T,
        g_fc,
        g_proj.T,
        pick_lanes(g_ext[1:7], rows),
        jnp.concatenate([pick_lanes(g_ext[7:9], piece), g_ext[0].reshape(piece, 4).T]),
    )
    return out, in_grad, reduced


def local(count, *args):
    (tokens, cotangent, segments, w_qkv, w_out, w_fc, w_proj, vec_norm, vec_split) = args[:9]
    firsts, seconds = args[9:15], args[15:21]
    masters = (w_qkv, w_out, w_fc, w_proj, vec_norm, vec_split)
    rows = w_fc.shape[0]
    piece = vec_split.shape[1]
    batches, length = tokens.shape[:2]
    total = batches * length
    t = tokens.reshape(total, D)
    cot = cotangent.reshape(total, D)
    seg = segments.reshape(total)
    place = jnp.arange(total)
    block = place // length
    allow = (
        (seg[:, None] == seg[None, :])
        & (block[:, None] == block[None, :])
        & (place[None, :] <= place[:, None])
    ).astype(F32)

    form = by_one if rows == 64 and 4 * piece == 128 else by_calls
    out, in_grad, reduced = form(
        count, t, cot, allow, w_qkv, w_out, w_fc, w_proj, vec_norm, vec_split
    )
    rates = rate_list()
    decays = (0.1, 0.1, 0.1, 0.1, 0.0, 0.0)
    updated = [
        adamw(masters[i], reduced[i], firsts[i], seconds[i], rates[i], decays[i])
        for i in range(6)
    ]
    return (
        out.reshape(tokens.shape),
        in_grad.reshape(tokens.shape),
        *(u[0] for u in updated),
        *(u[1] for u in updated),
        *(u[2] for u in updated),
    )


def solution(mesh):
    shards = (
        P(None, "dp", "mp"),
        P("mp", "dp"),
        P("dp", "mp"),
        P("mp", "dp"),
        P(None, "dp"),
        P(None, ("mp", "dp")),
    )
    rows = P(None, "dp", None)
    return jax.shard_map(
        functools.partial(local, mesh.shape["dp"]),
        mesh=mesh,
        in_specs=(rows, rows, P(None, "dp")) + shards * 3,
        out_specs=(rows, rows) + shards * 3,
        check_vma=False,
    )
```
